128 devices in a mesh: section: 2 (over core), gx: 16 (over x, z), gy: 4 (over y).
Axes of the slice: x: 4, y: 4, z: 4, core: 2. Of those that a mesh axis runs over, the one named last changes fastest.
Arguments:
- inputs: bfloat16 [2, 2048, 768], P(None, ('gx', 'gy')), may hold values from -6 to 6
- cotangent: bfloat16 [2, 2048, 768], P(None, ('gx', 'gy')), may hold values from -6 to 6
- ln1_gain: float32 [2, 768], P('section'), may hold values from 0.25 to 1.75
- ln1_bias: float32 [2, 768], P('section'), may hold values from -3 to 3
- w_qkv: bfloat16 [2, 768, 3, 768], P('section', 'gx', None, 'gy'), may hold values from -0.21875 to 0.21875
- b_qv: float32 [2, 2, 768], P('section', None, 'gy'), may hold values from -3 to 3
- w_out: bfloat16 [2, 768, 768], P('section', 'gy', 'gx'), may hold values from -0.875 to 0.875
- b_out: float32 [2, 768], P('section'), may hold values from -3 to 3
- ln2_gain: float32 [2, 768], P('section'), may hold values from 0.25 to 1.75
- ln2_bias: float32 [2, 768], P('section'), may hold values from -3 to 3
- w_up: bfloat16 [2, 768, 3072], P('section', 'gx', 'gy'), may hold values from -0.21875 to 0.21875
- b_up: float32 [2, 3072], P('section', 'gy'), may hold values from -3 to 3
- w_down: bfloat16 [2, 3072, 768], P('section', 'gy', 'gx'), may hold values from -0.109375 to 0.109375
- b_down: float32 [2, 768], P('section'), may hold values from -3 to 3
Outputs:
- activations: bfloat16 [2, 2, 2048, 768], P('section', None, ('gx', 'gy'))
- input_grads: bfloat16 [2, 2, 2048, 768], P('section', None, ('gx', 'gy'))
- grad_ln1_gain: float32 [2, 768], P('section')
- grad_ln1_bias: float32 [2, 768], P('section')
- grad_w_qkv: float32 [2, 768, 3, 768], P('section', 'gx', None, 'gy')
- grad_b_qv: float32 [2, 2, 768], P('section', None, 'gy')
- grad_w_out: float32 [2, 768, 768], P('section', 'gy', 'gx')
- grad_b_out: float32 [2, 768], P('section')
- grad_ln2_gain: float32 [2, 768], P('section')
- grad_ln2_bias: float32 [2, 768], P('section')
- grad_w_up: float32 [2, 768, 3072], P('section', 'gx', 'gy')
- grad_b_up: float32 [2, 3072], P('section', 'gy')
- grad_w_down: float32 [2, 3072, 768], P('section', 'gy', 'gx')
- grad_b_down: float32 [2, 768], P('section')
The draws below stay inside these ranges and needn't reach their ends.
All inputs are finite; a program needn't handle non-finite values.
Results may differ from the reference program's by a relative error of at most 0.02.
Values may be sent and summed in bfloat16 or wider, within the bound.
A program may use at most 128 MiB of HBM per device.

```python
import jax
import jax.numpy as jnp
from jax import lax

D = 768
HEADS = 12
HD = 64
FF = 3072
MICRO = 2
SEQ = 2048
LAYERS = 2


def steps_of(stream_key, shape, cuts, least, high):
    level = 1.0
    for axis_at, blocks in cuts:
        heights = jax.random.uniform(jax.random.fold_in(jax.random.fold_in(stream_key, 6), axis_at), (blocks,), jnp.float32, least / len(cuts), high / len(cuts))
        level = level * jnp.repeat(jnp.exp(heights), shape[axis_at] // blocks).reshape((-1,) + (1,) * (len(shape) - 1 - axis_at))
    return level


def scatter_about(stream_key, extent, deviation, most, split=(), kind=jnp.bfloat16):
    drawn = deviation * jax.random.normal(stream_key, extent, jnp.float32)
    if split:
        drawn = drawn * steps_of(stream_key, extent, split, -0.22, 0.18)
    return jnp.clip(drawn, -most, most).astype(kind)


def setup_inputs(seed: int = 0) -> dict:
    key_list = jax.random.split(jax.random.key(seed), 15)
    inputs = scatter_about(key_list[0], (MICRO, SEQ, D), 1.0, 6.0, ((1, 64),))
    cotangent = scatter_about(key_list[1], (MICRO, SEQ, D), 1.0, 6.0, ((1, 64),))
    ln1_gain = jnp.clip(1.0 + 0.15 * jax.random.normal(key_list[2], (LAYERS, D), jnp.float32), 0.25, 1.75)
    ln1_bias = scatter_about(key_list[3], (LAYERS, D), 0.3, 3.0, ((0, 2),), jnp.float32)
    w_qkv = scatter_about(key_list[4], (LAYERS, D, 3, D), D ** -0.5, 0.21875, ((0, 2), (1, 16), (3, 4)))
    b_qv = scatter_about(key_list[5], (LAYERS, 2, D), 0.3, 3.0, ((0, 2), (2, 4)), jnp.float32)
    w_out = scatter_about(key_list[6], (LAYERS, D, D), (D // 16) ** -0.5, 0.875, ((0, 2), (1, 4), (2, 16)))
    b_out = scatter_about(key_list[7], (LAYERS, D), 0.3, 3.0, ((0, 2),), jnp.float32)
    ln2_gain = jnp.clip(1.0 + 0.15 * jax.random.normal(key_list[8], (LAYERS, D), jnp.float32), 0.25, 1.75)
    ln2_bias = scatter_about(key_list[9], (LAYERS, D), 0.3, 3.0, ((0, 2),), jnp.float32)
    w_up = scatter_about(key_list[10], (LAYERS, D, FF), D ** -0.5, 0.21875, ((0, 2), (1, 16), (2, 4)))
    b_up = scatter_about(key_list[11], (LAYERS, FF), 0.5, 3.0, ((0, 2), (1, 4)), jnp.float32)
    w_down = scatter_about(key_list[12], (LAYERS, FF, D), FF ** -0.5, 0.109375, ((0, 2), (1, 4), (2, 16)))
    b_down = scatter_about(key_list[13], (LAYERS, D), 0.3, 3.0, ((0, 2),), jnp.float32)
    return dict(inputs=inputs, cotangent=cotangent, ln1_gain=ln1_gain, ln1_bias=ln1_bias, w_qkv=w_qkv, b_qv=b_qv, w_out=w_out, b_out=b_out, ln2_gain=ln2_gain, ln2_bias=ln2_bias, w_up=w_up, b_up=b_up, w_down=w_down, b_down=b_down)


HIGHEST = lax.Precision.HIGHEST
EPSILON = 1e-05

@jax.custom_vjp
def low(v):
    return lax.optimization_barrier(v.astype(jnp.bfloat16)).astype(jnp.float32)

@jax.custom_vjp
def low_back(v):
    return v

def low_keep(v):
    return (low(v), None)

def low_pass(kept, grad):
    return (grad,)

def back_keep(v):
    return (v, None)

def back_low(kept, grad):
    return (low(grad),)
low.defvjp(low_keep, low_pass)
low_back.defvjp(back_keep, back_low)

def layer_norm(values, gain, offset):
    average = lax.optimization_barrier(jnp.mean(values, axis=-1, keepdims=True))
    centered = values - average
    variance = lax.optimization_barrier(jnp.mean(centered * centered, axis=-1, keepdims=True))
    return centered * lax.rsqrt(variance + EPSILON) * gain + offset

def attend_block(block_start, queries, all_keys, all_values):
    scores = low_back(jnp.einsum('qhd,khd->hqk', queries, all_keys, precision=HIGHEST) * 0.125)
    query_pos = block_start + jnp.arange(queries.shape[0], dtype=jnp.int32)
    key_pos = jnp.arange(all_keys.shape[0], dtype=jnp.int32)
    allowed = key_pos[None, :] <= query_pos[:, None]
    scores = jnp.where(allowed[None], scores, -1e+30)
    largest = lax.optimization_barrier(jnp.max(scores, axis=-1, keepdims=True))
    weights = jnp.exp(scores - largest)
    totals = lax.optimization_barrier(jnp.sum(weights, axis=-1))
    summed = jnp.einsum('hqk,khd->qhd', low(weights), all_values, precision=HIGHEST)
    return summed / jnp.transpose(totals)[:, :, None]

def attention(queries, all_keys, all_values):
    block_rows = min(512, SEQ)
    block_count = SEQ // block_rows
    stacked = queries.reshape(block_count, block_rows, HEADS, HD)
    starts = jnp.arange(block_count, dtype=jnp.int32) * block_rows

    def one_block(pair):
        return attend_block(pair[0], pair[1], all_keys, all_values)
    result = lax.map(jax.checkpoint(one_block), (starts, stacked))
    return result.reshape(SEQ, D)

def layer(hidden_in, gain_one, offset_one, w_qkv, b_qv, w_out, b_out, gain_two, offset_two, w_up, b_up, w_down, b_down):
    normed = low(layer_norm(hidden_in, gain_one, offset_one))
    joined = jnp.einsum('td,dce->tce', normed, w_qkv, precision=HIGHEST)
    queries = low_back(low(joined[:, 0] + b_qv[0]))
    keys_in = low_back(low(joined[:, 1]))
    values_in = low_back(low(joined[:, 2] + b_qv[1]))
    heads_shape = (SEQ, HEADS, HD)
    attended = attention(queries.reshape(heads_shape), keys_in.reshape(heads_shape), values_in.reshape(heads_shape))
    mixed = low_back(low(attended))
    middle = hidden_in + low_back(jnp.dot(mixed, w_out, precision=HIGHEST)) + b_out
    normed_two = low(layer_norm(middle, gain_two, offset_two))
    upward = low_back(jnp.dot(normed_two, w_up, precision=HIGHEST) + b_up)
    active = low(jax.nn.gelu(upward, approximate=True))
    return low(middle + jnp.dot(active, w_down, precision=HIGHEST) + b_down)

def reference(inputs, cotangent, ln1_gain, ln1_bias, w_qkv, b_qv, w_out, b_out, ln2_gain, ln2_bias, w_up, b_up, w_down, b_down):
    params = tuple((array.astype(jnp.float32) for array in (ln1_gain, ln1_bias, w_qkv, b_qv, w_out, b_out, ln2_gain, ln2_bias, w_up, b_up, w_down, b_down)))
    start_rows = inputs.astype(jnp.float32)
    nudges = jnp.zeros((MICRO, LAYERS, SEQ, D), jnp.float32)

    def forward(extra_all, weights_all):

        def one_micro(pair):
            sequence, extra = pair
            outputs = []
            current = sequence + extra[0]
            for layer_index in range(LAYERS):
                if layer_index > 0:
                    current = low_back(current) + extra[layer_index]
                current = layer(current, *[weight[layer_index] for weight in weights_all])
                outputs.append(current)
            return jnp.stack(outputs)
        return lax.map(one_micro, (start_rows, extra_all))
    results, pullback = jax.vjp(forward, nudges, params)
    seed_grads = jnp.zeros_like(results).at[:, LAYERS - 1].set(cotangent.astype(jnp.float32))
    nudge_grads, param_grads = pullback(seed_grads)
    activations = jnp.transpose(results, (1, 0, 2, 3)).astype(jnp.bfloat16)
    input_grads = jnp.transpose(nudge_grads, (1, 0, 2, 3)).astype(jnp.bfloat16)
    return (activations, input_grads, param_grads[0], param_grads[1], param_grads[2], param_grads[3], param_grads[4], param_grads[5], param_grads[6], param_grads[7], param_grads[8], param_grads[9], param_grads[10], param_grads[11])
```

```python
import jax
import jax.numpy as jnp
from jax import lax
from jax.experimental import pallas as pl
from jax.experimental.pallas import tpu as pltpu
from jax.sharding import PartitionSpec as P

HD = 64
EPSILON = 1e-05
MASKED = -1e30
MESH = pl.DeviceIdType.MESH
F32 = jnp.float32
BF16 = jnp.bfloat16

ROWS = 32
FULL = 128
D = 768
CHUNK = 512
HEADS = 3
STACK = HEADS * FULL

UP = slice(0, 768)
DOWN = slice(768, 1536)
KV = slice(1536, 1920)
QUERY = slice(1920, 2176)
OUT = slice(2048, 2304)
QUERY_OUT = slice(1920, 2304)
COLUMNS = 2304
HALF = COLUMNS // 2
SHARD = 48
SEMS = 200


def dot_nn(a, b):
    return lax.dot_general(a, b, (((1,), (0,)), ((), ())), preferred_element_type=F32)


def dot_nt(a, b):
    return lax.dot_general(a, b, (((1,), (1,)), ((), ())), preferred_element_type=F32)


def dot_tn(a, b):
    return lax.dot_general(a, b, (((0,), (0,)), ((), ())), preferred_element_type=F32)


def norm_parts(values, gain, offset):
    average = jnp.mean(values, axis=-1, keepdims=True)
    centered = values - average
    variance = jnp.mean(centered * centered, axis=-1, keepdims=True)
    factor = lax.rsqrt(variance + EPSILON)
    unit_rows = centered * factor
    return (unit_rows * gain + offset, unit_rows, factor)


def norm_back(grad_rows, unit_rows, factor, gain):
    scaled = grad_rows * gain
    first_mean = jnp.mean(scaled, axis=-1, keepdims=True)
    second_mean = jnp.mean(scaled * unit_rows, axis=-1, keepdims=True)
    return factor * (scaled - first_mean - unit_rows * second_mean)


def gelu_parts(values):
    scale = 0.7978845608028654
    inner = scale * (values + 0.044715 * values * values * values)
    bent = jnp.tanh(inner)
    active = 0.5 * values * (1.0 + bent)
    slope = 0.5 * (1.0 + bent) + 0.5 * values * (1.0 - bent * bent) * scale * (
        1.0 + 3.0 * 0.044715 * values * values
    )
    return active, slope


def column_sum(values):
    return jnp.sum(values, axis=0, keepdims=True)


def head_mask(head, first):
    lane = lax.broadcasted_iota(jnp.int32, (FULL, 256), 1)
    low = first + HD * head
    return jnp.logical_and(lane >= low, lane < low + HD)


def spread_heads(values, first):
    return jnp.concatenate(
        [jnp.where(head_mask(head, first), values, 0.0) for head in range(HEADS)], axis=0
    )


def join_heads(stacked, first):
    total = jnp.zeros((FULL, 256), F32)
    for head in range(HEADS):
        part = stacked[head * FULL : (head + 1) * FULL]
        total = total + jnp.where(head_mask(head, first), part, 0.0)
    return total


class Links:
    def __init__(self, send_sems, recv_sems):
        self.send_sems, self.recv_sems = send_sems, recv_sems
        self.count = 0
        self.sent = []
        self.section = lax.axis_index("section")
        self.row = lax.axis_index("gx")
        self.y = lax.axis_index("gy")
        self.x = self.row // 4
        self.z = self.row % 4

    def near(self, axis, steps):
        if axis == "s":
            return 1 - self.section
        return (getattr(self, axis) + (steps + 4)) % 4

    def device(self, axis, steps):
        s, x, z, y = self.section, self.x, self.z, self.y
        there = self.near(axis, steps)
        if axis == "s":
            s = there
        elif axis == "x":
            x = there
        elif axis == "z":
            z = there
        else:
            y = there
        return (s, x * 4 + z, y)

    def exchange(self, axis, steps, source, target, landing):
        index = self.count
        self.count += 1
        sems = (self.send_sems.at[index], self.recv_sems.at[index])
        copy = pltpu.make_async_remote_copy(
            source, target, *sems, device_id=self.device(axis, steps), device_id_type=MESH
        )
        copy.start()
        self.sent.append(copy)
        arrival = pltpu.make_async_remote_copy(
            landing, landing, *sems, device_id=self.device(axis, -steps), device_id_type=MESH
        )
        return arrival.wait_recv

    def barrier(self):
        barrier = pltpu.get_barrier_semaphore()
        peers = [("s", 1)] + [(axis, steps) for axis in "xyz" for steps in (1, 2, 3)]
        for axis, steps in peers:
            pl.semaphore_signal(
                barrier, inc=1, device_id=self.device(axis, steps), device_id_type=MESH
            )
        pl.semaphore_wait(barrier, len(peers))

    def finish(self):
        for copy in self.sent:
            copy.wait_send()
        self.sent = []


def wait_all(waits):
    for wait in waits:
        wait()


def gather_y(links, buffer):
    y = links.y
    return [
        links.exchange("y", steps, buffer.at[y], buffer.at[y], buffer.at[links.near("y", -steps)])
        for steps in (1, 3, 2)
    ]


def scatter_y(links, outgoing, incoming, partial):
    y = links.y
    outgoing[...] = partial.astype(BF16).reshape(4, ROWS, D)
    waits = [
        links.exchange(
            "y",
            steps,
            outgoing.at[links.near("y", steps)],
            incoming.at[y],
            incoming.at[links.near("y", -steps)],
        )
        for steps in (2, 1, 3)
    ]
    incoming[y] = outgoing[y]
    return waits


def sum_slots(buffer):
    total = buffer[0].astype(F32)
    for slot in range(1, 4):
        total = total + buffer[slot].astype(F32)
    return total


def kernel(
    inputs,
    cotangent,
    own_weights,
    own_params,
    activations,
    input_grads,
    weight_grads,
    param_grads,
    send_sems,
    recv_sems,
    weights,
    params,
    normed_one,
    normed_two,
    grad_outs,
    grad_branches,
    scatter_out,
    scatter_in,
    pairs,
    scores,
    probs,
    queries,
    totals,
    attended,
    hidden,
    middles,
    actives,
    slopes,
    pair_grads,
    pair_in_a,
    pair_in_b,
    pair_mid_a,
    pair_mid_b,
    pair_end_a,
    pair_end_b,
    grads,
    grads_cross,
    grads_in_a,
    grads_in_b,
    grads_mid_a,
    grads_mid_b,
    grads_end_a,
    grads_end_b,
    sums,
    sums_cross,
    sums_y,
    sums_z,
    sums_x,
    outputs,
    output_cross,
    in_grads,
    in_grad_cross,
):
    links = Links(send_sems, recv_sems)
    s, x, z, y, row = links.section, links.x, links.z, links.y, links.row
    other = 1 - s
    side_a, side_b = pl.ds(0, HALF), pl.ds(HALF, HALF)
    links.barrier()

    params[s] = own_params[...]
    params_wait = links.exchange("s", 1, params.at[s], params.at[s], params.at[other])

    weights[s, x, z] = own_weights[...]
    first_a = [
        links.exchange(
            "z",
            steps,
            weights.at[s, x, z, :, side_a],
            weights.at[s, x, z, :, side_a],
            weights.at[s, x, links.near("z", -steps), :, side_a],
        )
        for steps in (1, 3, 2)
    ]
    first_b = [
        links.exchange(
            "x",
            steps,
            weights.at[s, x, z, :, side_b],
            weights.at[s, x, z, :, side_b],
            weights.at[s, links.near("x", -steps), z, :, side_b],
        )
        for steps in (1, 3, 2)
    ]

    params_wait()

    def norm_rows(layer, current):
        hidden[layer] = current
        normed, _, _ = norm_parts(current, params[layer, 0:1, :], params[layer, 1:2, :])
        normed_one[layer, y] = normed.astype(BF16)
        return gather_y(links, normed_one.at[layer])

    normed_waits = norm_rows(0, inputs[s].astype(F32))

    wait_all(first_a)
    second_a = [
        links.exchange(
            "x",
            steps,
            weights.at[s, x, :, :, side_a],
            weights.at[s, x, :, :, side_a],
            weights.at[s, links.near("x", -steps), :, :, side_a],
        )
        for steps in (1, 3, 2)
    ]
    wait_all(first_b)
    second_b = [
        links.exchange(
            "z",
            steps,
            weights.at[s, :, z, :, side_b],
            weights.at[s, :, z, :, side_b],
            weights.at[s, :, links.near("z", -steps), :, side_b],
        )
        for steps in (1, 3, 2)
    ]
    crossings = [
        links.exchange(
            "s",
            1,
            weights.at[s, x, :, :, side_a],
            weights.at[s, x, :, :, side_a],
            weights.at[other, x, :, :, side_a],
        ),
        links.exchange(
            "s",
            1,
            weights.at[s, :, z, :, side_b],
            weights.at[s, :, z, :, side_b],
            weights.at[other, :, z, :, side_b],
        ),
    ]
    for index, steps in enumerate((1, 3, 2)):
        second_a[index]()
        came = links.near("x", -steps)
        crossings.append(
            links.exchange(
                "s",
                1,
                weights.at[s, came, :, :, side_a],
                weights.at[s, came, :, :, side_a],
                weights.at[other, came, :, :, side_a],
            )
        )
        second_b[index]()
        came = links.near("z", -steps)
        crossings.append(
            links.exchange(
                "s",
                1,
                weights.at[s, :, came, :, side_b],
                weights.at[s, :, came, :, side_b],
                weights.at[other, :, came, :, side_b],
            )
        )
    wait_all(crossings)

    def matrix(layer, columns):
        width = columns.stop - columns.start
        return weights[layer, :, :, :, columns].reshape(D, width)

    def forward(layer, normed_waits):
        wait_all(normed_waits)
        normed = normed_one[layer].reshape(FULL, D)
        pair = dot_nn(normed, matrix(layer, KV)) + params[layer, 7:8, 0:384]
        pairs[layer, x, z] = pair.astype(BF16)
        own = pairs.at[layer]
        low, high = pl.ds(0, 64), pl.ds(64, 64)
        pair_first_a = [
            links.exchange(
                "z",
                steps,
                own.at[x, z, low],
                own.at[x, z, low],
                own.at[x, links.near("z", -steps), low],
            )
            for steps in (1, 3, 2)
        ]
        pair_first_b = [
            links.exchange(
                "x",
                steps,
                own.at[x, z, high],
                own.at[x, z, high],
                own.at[links.near("x", -steps), z, high],
            )
            for steps in (1, 3, 2)
        ]
        query = dot_nn(normed, matrix(layer, QUERY)) + params[layer, 7:8, 384:640]
        query = query.astype(BF16).astype(F32) * 0.125
        queries[layer] = spread_heads(query, 0).astype(BF16)
        wait_all(pair_first_a)
        pair_second_a = [
            links.exchange(
                "x",
                steps,
                own.at[x, :, low],
                own.at[x, :, low],
                own.at[links.near("x", -steps), :, low],
            )
            for steps in (1, 3, 2)
        ]
        wait_all(pair_first_b)
        pair_second_b = [
            links.exchange(
                "z",
                steps,
                own.at[:, z, high],
                own.at[:, z, high],
                own.at[:, links.near("z", -steps), high],
            )
            for steps in (1, 3, 2)
        ]
        wait_all(pair_second_a)
        wait_all(pair_second_b)

        stacked = queries[layer]
        position = lax.broadcasted_iota(jnp.int32, (STACK, CHUNK), 0) % FULL + row * FULL
        column = lax.broadcasted_iota(jnp.int32, (STACK, CHUNK), 1)

        def find_top(chunk, running):
            keys = pairs[layer, chunk, :, :, 0:256].reshape(CHUNK, 256)
            raw = dot_nt(stacked, keys)
            raw = jnp.where(column + chunk * CHUNK <= position, raw, MASKED)
            scores[chunk] = raw
            return jnp.maximum(running, jnp.max(raw, axis=1, keepdims=True))

        top = lax.fori_loop(0, x + 1, find_top, jnp.full((STACK, 1), MASKED, F32))

        def add_chunk(chunk, carry):
            total, summed = carry
            weight = jnp.exp(scores[chunk] - top)
            rounded = weight.astype(BF16)
            probs[layer, chunk] = rounded
            values = pairs[layer, chunk, :, :, 128:384].reshape(CHUNK, 256)
            return (
                total + jnp.sum(weight, axis=1, keepdims=True),
                summed + dot_nn(rounded, values),
            )

        total, summed = lax.fori_loop(
            0, x + 1, add_chunk, (jnp.zeros((STACK, 1), F32), jnp.zeros((STACK, 256), F32))
        )
        totals[layer] = total
        attention = join_heads(summed / total, HD)
        attended[layer] = attention
        partial = dot_nt(attention.astype(BF16), matrix(layer, OUT))
        wait_all(scatter_y(links, scatter_out.at[layer, 0], scatter_in.at[layer, 0], partial))
        middle = hidden[layer] + sum_slots(scatter_in.at[layer, 0]) + params[layer, 2:3, :]
        middles[layer] = middle
        second, _, _ = norm_parts(middle, params[layer, 3:4, :], params[layer, 4:5, :])
        normed_two[layer, y] = second.astype(BF16)
        wait_all(gather_y(links, normed_two.at[layer]))
        upward = (
            dot_nn(normed_two[layer].reshape(FULL, D), matrix(layer, UP)) + params[layer, 6:7, :]
        )
        active, slope = gelu_parts(upward)
        actives[layer] = active.astype(BF16)
        slopes[layer] = slope
        partial = dot_nt(actives[layer], matrix(layer, DOWN))
        wait_all(scatter_y(links, scatter_out.at[layer, 1], scatter_in.at[layer, 1], partial))
        result = middle + sum_slots(scatter_in.at[layer, 1]) + params[layer, 5:6, :]
        outputs[layer] = result.astype(BF16)

    forward(0, normed_waits)
    forward(1, norm_rows(1, outputs[0].astype(F32)))
    output_wait = links.exchange("s", 1, outputs.at[other], output_cross, output_cross)

    def backward(layer, grad_rows):
        grad_outs[layer, y] = grad_rows
        waits = gather_y(links, grad_outs.at[layer])
        sums[layer, 5:6, :] = column_sum(grad_rows.astype(F32))
        gain_one, gain_two = params[layer, 0:1, :], params[layer, 3:4, :]
        _, unit_one, factor_one = norm_parts(hidden[layer], gain_one, gain_one)
        _, unit_two, factor_two = norm_parts(middles[layer], gain_two, gain_two)
        wait_all(waits)
        grad_full = grad_outs[layer].reshape(FULL, D)
        grad_up = (dot_nn(grad_full, matrix(layer, DOWN)) * slopes[layer]).astype(BF16)
        partial = dot_nt(grad_up, matrix(layer, UP))
        waits = scatter_y(links, scatter_out.at[layer, 2], scatter_in.at[layer, 2], partial)
        down_grad = dot_tn(grad_full, actives[layer])
        grads[layer, :, :, :, DOWN] = down_grad.astype(BF16).reshape(4, 4, SHARD, D)
        up_grad = dot_tn(normed_two[layer].reshape(FULL, D), grad_up)
        grads[layer, :, :, :, UP] = up_grad.astype(BF16).reshape(4, 4, SHARD, D)
        sums[layer, 6:7, :] = column_sum(grad_up.astype(F32))
        wait_all(waits)
        grad_two = sum_slots(scatter_in.at[layer, 2])
        grad_middle = grad_rows.astype(F32) + norm_back(grad_two, unit_two, factor_two, gain_two)
        grad_branches[layer, y] = grad_middle.astype(BF16)
        waits = gather_y(links, grad_branches.at[layer])
        sums[layer, 2:3, :] = column_sum(grad_middle)
        sums[layer, 3:4, :] = column_sum(grad_two * unit_two)
        sums[layer, 4:5, :] = column_sum(grad_two)
        wait_all(waits)
        branch_full = grad_branches[layer].reshape(FULL, D)
        grad_mixed = dot_nn(branch_full, matrix(layer, OUT)).astype(BF16).astype(F32)
        stacked_grad = spread_heads(grad_mixed, HD)
        delta = jnp.sum(spread_heads(grad_mixed * attended[layer], HD), axis=1, keepdims=True)
        inverse = 1.0 / totals[layer]
        scaled_grad = (stacked_grad * inverse).astype(BF16)
        stacked_grad = stacked_grad.astype(BF16)
        stacked = queries[layer]

        def chunk_back(chunk, summed):
            keys = pairs[layer, chunk, :, :, 0:256].reshape(CHUNK, 256)
            values = pairs[layer, chunk, :, :, 128:384].reshape(CHUNK, 256)
            weight = probs[layer, chunk]
            products = dot_nt(stacked_grad, values)
            score_grad = (weight.astype(F32) * (products - delta) * inverse).astype(BF16)
            key_grad = dot_tn(score_grad, stacked)
            value_grad = dot_tn(weight, scaled_grad)
            joined = jnp.concatenate(
                [
                    key_grad[:, :128],
                    key_grad[:, 128:] + value_grad[:, :128],
                    value_grad[:, 128:],
                ],
                axis=1,
            )
            pair_grads[layer, chunk] = joined.astype(BF16).reshape(4, FULL, 384)
            return summed + dot_nn(score_grad, keys)

        def chunk_clear(chunk, carry):
            pair_grads[layer, chunk] = jnp.zeros((4, FULL, 384), BF16)
            return carry

        lax.fori_loop(x + 1, 4, chunk_clear, 0)
        query_sum = lax.fori_loop(0, x + 1, chunk_back, jnp.zeros((STACK, 256), F32))
        own = pair_grads.at[layer]
        low, high = pl.ds(0, 64), pl.ds(64, 64)
        waits_a = [
            links.exchange(
                "x",
                steps,
                own.at[links.near("x", steps), :, low],
                pair_in_a.at[layer, x],
                pair_in_a.at[layer, links.near("x", -steps)],
            )
            for steps in (2, 1, 3)
        ]
        waits_b = [
            links.exchange(
                "z",
                steps,
                own.at[:, links.near("z", steps), high],
                pair_in_b.at[layer, z],
                pair_in_b.at[layer, links.near("z", -steps)],
            )
            for steps in (2, 1, 3)
        ]
        pair_in_a[layer, x] = pair_grads[layer, x, :, 0:64]
        pair_in_b[layer, z] = pair_grads[layer, :, z, 64:128]
        grad_query = (join_heads(query_sum, 0) * 0.125).astype(BF16)
        normed = normed_one[layer].reshape(FULL, D)
        query_grad = dot_tn(normed, grad_query)
        out_grad = dot_tn(branch_full, attended[layer].astype(BF16))
        joined = jnp.concatenate(
            [
                query_grad[:, :128],
                query_grad[:, 128:] + out_grad[:, :128],
                out_grad[:, 128:],
            ],
            axis=1,
        )
        grads[layer, :, :, :, QUERY_OUT] = joined.astype(BF16).reshape(4, 4, SHARD, 384)
        partial = dot_nt(grad_query, matrix(layer, QUERY))
        wait_all(waits_a)
        pair_mid_a[layer] = sum_slots(pair_in_a.at[layer]).astype(BF16)
        waits_a = [
            links.exchange(
                "z",
                steps,
                pair_mid_a.at[layer, links.near("z", steps)],
                pair_end_a.at[layer, z],
                pair_end_a.at[layer, links.near("z", -steps)],
            )
            for steps in (2, 1, 3)
        ]
        pair_end_a[layer, z] = pair_mid_a[layer, z]
        wait_all(waits_b)
        pair_mid_b[layer] = sum_slots(pair_in_b.at[layer]).astype(BF16)
        waits_b = [
            links.exchange(
                "x",
                steps,
                pair_mid_b.at[layer, links.near("x", steps)],
                pair_end_b.at[layer, x],
                pair_end_b.at[layer, links.near("x", -steps)],
            )
            for steps in (2, 1, 3)
        ]
        pair_end_b[layer, x] = pair_mid_b[layer, x]
        wait_all(waits_a)
        wait_all(waits_b)
        grad_pair = jnp.concatenate(
            [sum_slots(pair_end_a.at[layer]), sum_slots(pair_end_b.at[layer])], axis=0
        ).astype(BF16)
        partial = partial + dot_nt(grad_pair, matrix(layer, KV))
        waits = scatter_y(links, scatter_out.at[layer, 3], scatter_in.at[layer, 3], partial)
        pair_weight_grad = dot_tn(normed, grad_pair)
        grads[layer, :, :, :, KV] = pair_weight_grad.astype(BF16).reshape(4, 4, SHARD, 384)
        sums[layer, 7:8, :] = jnp.concatenate(
            [
                column_sum(grad_pair.astype(F32)),
                column_sum(grad_query.astype(F32)),
                jnp.zeros((1, 128), F32),
            ],
            axis=1,
        )
        wait_all(waits)
        grad_one = sum_slots(scatter_in.at[layer, 3])
        sums[layer, 0:1, :] = column_sum(grad_one * unit_one)
        sums[layer, 1:2, :] = column_sum(grad_one)
        grad_input = grad_middle + norm_back(grad_one, unit_one, factor_one, gain_one)
        in_grads[layer] = grad_input.astype(BF16)

    backward(1, cotangent[s])
    backward(0, in_grads[1])
    in_grad_wait = links.exchange("s", 1, in_grads.at[other], in_grad_cross, in_grad_cross)

    cross_wait = links.exchange("s", 1, grads.at[other], grads_cross, grads_cross)
    sums_wait = links.exchange("s", 1, sums.at[other], sums_cross, sums_cross)
    sums_wait()
    sums_y[y] = sums[s] + sums_cross[...]
    waits = gather_y(links, sums_y)
    wait_all(waits)
    sums_z[z] = jnp.concatenate([sum_slots(sums_y)[0:6], sums_y[y, 6:8, :]], axis=0)
    z_waits = [
        links.exchange(
            "z", steps, sums_z.at[z], sums_z.at[z], sums_z.at[links.near("z", -steps)]
        )
        for steps in (1, 3, 2)
    ]
    cross_wait()

    def add_cross(step, carry):
        mine = grads[s, step].astype(F32)
        grads[s, step] = (mine + grads_cross[step].astype(F32)).astype(BF16)
        return carry

    lax.fori_loop(0, 4, add_cross, 0)
    waits_a = [
        links.exchange(
            "x",
            steps,
            grads.at[s, links.near("x", steps), :, :, side_a],
            grads_in_a.at[x],
            grads_in_a.at[links.near("x", -steps)],
        )
        for steps in (2, 1, 3)
    ]
    waits_b = [
        links.exchange(
            "z",
            steps,
            grads.at[s, :, links.near("z", steps), :, side_b],
            grads_in_b.at[z],
            grads_in_b.at[links.near("z", -steps)],
        )
        for steps in (2, 1, 3)
    ]
    grads_in_a[x] = grads[s, x, :, :, 0:HALF]
    grads_in_b[z] = grads[s, :, z, :, HALF:COLUMNS]
    wait_all(z_waits)
    sums_x[x] = sum_slots(sums_z)
    x_waits = [
        links.exchange(
            "x", steps, sums_x.at[x], sums_x.at[x], sums_x.at[links.near("x", -steps)]
        )
        for steps in (1, 3, 2)
    ]
    output_wait()
    activations[s] = outputs[s]
    activations[other] = output_cross[...]
    in_grad_wait()
    input_grads[s] = in_grads[s]
    input_grads[other] = in_grad_cross[...]
    wait_all(waits_a)
    grads_mid_a[...] = sum_slots(grads_in_a).astype(BF16)
    waits_a = [
        links.exchange(
            "z",
            steps,
            grads_mid_a.at[links.near("z", steps)],
            grads_end_a.at[z],
            grads_end_a.at[links.near("z", -steps)],
        )
        for steps in (2, 1, 3)
    ]
    grads_end_a[z] = grads_mid_a[z]
    wait_all(waits_b)
    grads_mid_b[...] = sum_slots(grads_in_b).astype(BF16)
    waits_b = [
        links.exchange(
            "x",
            steps,
            grads_mid_b.at[links.near("x", steps)],
            grads_end_b.at[x],
            grads_end_b.at[links.near("x", -steps)],
        )
        for steps in (2, 1, 3)
    ]
    grads_end_b[x] = grads_mid_b[x]
    wait_all(x_waits)
    param_grads[...] = sum_slots(sums_x)
    wait_all(waits_a)
    weight_grads[:, 0:HALF] = sum_slots(grads_end_a)
    wait_all(waits_b)
    weight_grads[:, HALF:COLUMNS] = sum_slots(grads_end_b)
    links.finish()


def scratch_shapes():
    def low(*shape):
        return pltpu.VMEM(shape, BF16)

    def full(*shape):
        return pltpu.VMEM(shape, F32)

    return [
        pltpu.SemaphoreType.DMA((SEMS,)),
        pltpu.SemaphoreType.DMA((SEMS,)),
        low(2, 4, 4, SHARD, COLUMNS),
        full(2, 8, D),
        low(2, 4, ROWS, D),
        low(2, 4, ROWS, D),
        low(2, 4, ROWS, D),
        low(2, 4, ROWS, D),
        low(2, 4, 4, ROWS, D),
        low(2, 4, 4, ROWS, D),
        low(2, 4, 4, FULL, 384),
        full(4, STACK, CHUNK),
        low(2, 4, STACK, CHUNK),
        low(2, STACK, 256),
        full(2, STACK, 1),
        full(2, FULL, 256),
        full(2, ROWS, D),
        full(2, ROWS, D),
        low(2, FULL, D),
        full(2, FULL, D),
        low(2, 4, 4, FULL, 384),
        low(2, 4, 4, 64, 384),
        low(2, 4, 4, 64, 384),
        low(2, 4, 64, 384),
        low(2, 4, 64, 384),
        low(2, 4, 64, 384),
        low(2, 4, 64, 384),
        low(2, 4, 4, SHARD, COLUMNS),
        low(4, 4, SHARD, COLUMNS),
        low(4, 4, SHARD, HALF),
        low(4, 4, SHARD, HALF),
        low(4, SHARD, HALF),
        low(4, SHARD, HALF),
        low(4, SHARD, HALF),
        low(4, SHARD, HALF),
        full(2, 8, D),
        full(8, D),
        full(4, 8, D),
        full(4, 8, D),
        full(4, 8, D),
        low(2, ROWS, D),
        low(ROWS, D),
        low(2, ROWS, D),
        low(ROWS, D),
    ]


def local(
    inputs,
    cotangent,
    ln1_gain,
    ln1_bias,
    w_qkv,
    b_qv,
    w_out,
    b_out,
    ln2_gain,
    ln2_bias,
    w_up,
    b_up,
    w_down,
    b_down,
):
    packed = jnp.concatenate(
        [
            w_up[0],
            w_down[0].T,
            w_qkv[0, :, 1],
            w_qkv[0, :, 2],
            w_qkv[0, :, 0],
            w_out[0].T,
        ],
        axis=1,
    )
    biases = jnp.concatenate(
        [jnp.zeros((1, 192), F32), b_qv[:, 1], b_qv[:, 0], jnp.zeros((1, 192), F32)], axis=1
    )
    params = jnp.concatenate(
        [ln1_gain, ln1_bias, b_out, ln2_gain, ln2_bias, b_down, b_up, biases], axis=0
    )
    whole = pl.BlockSpec(memory_space=pltpu.VMEM)
    acts, in_grads, weight_grads, sums = pl.pallas_call(
        kernel,
        name="layers",
        out_shape=(
            jax.ShapeDtypeStruct((2, ROWS, D), BF16),
            jax.ShapeDtypeStruct((2, ROWS, D), BF16),
            jax.ShapeDtypeStruct((SHARD, COLUMNS), F32),
            jax.ShapeDtypeStruct((8, D), F32),
        ),
        in_specs=[whole] * 4,
        out_specs=(whole,) * 4,
        scratch_shapes=scratch_shapes(),
        compiler_params=pltpu.CompilerParams(
            collective_id=0, has_side_effects=True, vmem_limit_bytes=60 * 2**20
        ),
    )(inputs, cotangent, packed, params)
    qkv_grad = jnp.stack(
        [weight_grads[:, 1920:2112], weight_grads[:, 1536:1728], weight_grads[:, 1728:1920]],
        axis=1,
    )
    return (
        acts[None],
        in_grads[None],
        sums[0:1],
        sums[1:2],
        qkv_grad[None],
        jnp.stack([sums[7, 384:576], sums[7, 192:384]])[None],
        weight_grads[:, 2112:2304].T[None],
        sums[2:3],
        sums[3:4],
        sums[4:5],
        weight_grads[:, UP][None],
        sums[6:7],
        weight_grads[:, DOWN].T[None],
        sums[5:6],
    )


def solution(mesh):
    rows = P(None, ("gx", "gy"), None)
    vector = P("section", None)
    qkv = P("section", "gx", None, "gy")
    bias_qv = P("section", None, "gy")
    out = P("section", "gy", "gx")
    up = P("section", "gx", "gy")
    hidden = P("section", "gy")
    sharded = (vector, vector, qkv, bias_qv, out, vector, vector, vector, up, hidden, out, vector)
    layer_rows = P("section", None, ("gx", "gy"), None)
    return jax.shard_map(
        local,
        mesh=mesh,
        in_specs=(rows, rows) + sharded,
        out_specs=(layer_rows, layer_rows) + sharded,
        check_vma=False,
    )
```

```python
import jax
import jax.numpy as jnp
from jax import lax
from jax.experimental import pallas as pl
from jax.experimental.pallas import tpu as pltpu
from jax.sharding import PartitionSpec as P

HD = 64
EPSILON = 1e-05
MASKED = -1e30
MESH = pl.DeviceIdType.MESH
F32 = jnp.float32
BF16 = jnp.bfloat16

ROWS = 32
FULL = 128
D = 768
CHUNK = 512
HEADS = 3
STACK = HEADS * FULL

WIDE = 768
NARROW = 384
SHARD = 48
SEMS = 240


def dot_nn(a, b):
    return lax.dot_general(a, b, (((1,), (0,)), ((), ())), preferred_element_type=F32)


def dot_nt(a, b):
    return lax.dot_general(a, b, (((1,), (1,)), ((), ())), preferred_element_type=F32)


def dot_tn(a, b):
    return lax.dot_general(a, b, (((0,), (0,)), ((), ())), preferred_element_type=F32)


def norm_parts(values, gain, offset):
    average = jnp.mean(values, axis=-1, keepdims=True)
    centered = values - average
    variance = jnp.mean(centered * centered, axis=-1, keepdims=True)
    factor = lax.rsqrt(variance + EPSILON)
    unit_rows = centered * factor
    return (unit_rows * gain + offset, unit_rows, factor)


def norm_back(grad_rows, unit_rows, factor, gain):
    scaled = grad_rows * gain
    first_mean = jnp.mean(scaled, axis=-1, keepdims=True)
    second_mean = jnp.mean(scaled * unit_rows, axis=-1, keepdims=True)
    return factor * (scaled - first_mean - unit_rows * second_mean)


def gelu_parts(values):
    scale = 0.7978845608028654
    inner = scale * (values + 0.044715 * values * values * values)
    bent = jnp.tanh(inner)
    active = 0.5 * values * (1.0 + bent)
    slope = 0.5 * (1.0 + bent) + 0.5 * values * (1.0 - bent * bent) * scale * (
        1.0 + 3.0 * 0.044715 * values * values
    )
    return active, slope


def column_sum(values):
    return jnp.sum(values, axis=0, keepdims=True)


def head_mask(head, first):
    lane = lax.broadcasted_iota(jnp.int32, (FULL, 256), 1)
    low = first + HD * head
    return jnp.logical_and(lane >= low, lane < low + HD)


def spread_heads(values, first):
    return jnp.concatenate(
        [jnp.where(head_mask(head, first), values, 0.0) for head in range(HEADS)], axis=0
    )


def join_heads(stacked, first):
    total = jnp.zeros((FULL, 256), F32)
    for head in range(HEADS):
        part = stacked[head * FULL : (head + 1) * FULL]
        total = total + jnp.where(head_mask(head, first), part, 0.0)
    return total


class Links:
    def __init__(self, send_sems, recv_sems):
        self.send_sems, self.recv_sems = send_sems, recv_sems
        self.count = 0
        self.sent = []
        self.section = lax.axis_index("section")
        self.row = lax.axis_index("gx")
        self.y = lax.axis_index("gy")
        self.x = self.row // 4
        self.z = self.row % 4

    def near(self, axis, steps):
        if axis == "s":
            return 1 - self.section
        return (getattr(self, axis) + (steps + 4)) % 4

    def place(self, first, second):
        s = self.section
        x = (self.x + (first + 4) * s + (second + 4) * (1 - s)) % 4
        z = (self.z + (first + 4) * (1 - s) + (second + 4) * s) % 4
        return x, z

    def device(self, axis, steps):
        s, x, z, y = self.section, self.x, self.z, self.y
        if axis == "first":
            x, z = self.place(steps, 0)
            return (s, x * 4 + z, y)
        if axis == "second":
            x, z = self.place(0, steps)
            return (s, x * 4 + z, y)
        there = self.near(axis, steps)
        if axis == "s":
            s = there
        elif axis == "x":
            x = there
        elif axis == "z":
            z = there
        else:
            y = there
        return (s, x * 4 + z, y)

    def exchange(self, axis, steps, source, target, landing):
        index = self.count
        self.count += 1
        sems = (self.send_sems.at[index], self.recv_sems.at[index])
        copy = pltpu.make_async_remote_copy(
            source, target, *sems, device_id=self.device(axis, steps), device_id_type=MESH
        )
        copy.start()
        self.sent.append(copy)
        arrival = pltpu.make_async_remote_copy(
            landing, landing, *sems, device_id=self.device(axis, -steps), device_id_type=MESH
        )
        return arrival.wait_recv

    def barrier(self):
        barrier = pltpu.get_barrier_semaphore()
        peers = [("s", 1)] + [(axis, steps) for axis in "xyz" for steps in (1, 2, 3)]
        for axis, steps in peers:
            pl.semaphore_signal(
                barrier, inc=1, device_id=self.device(axis, steps), device_id_type=MESH
            )
        pl.semaphore_wait(barrier, len(peers))

    def finish(self):
        for copy in self.sent:
            copy.wait_send()
        self.sent = []


def wait_all(waits):
    for wait in waits:
        wait()


def gather_y(links, buffer):
    y = links.y
    return [
        links.exchange("y", steps, buffer.at[y], buffer.at[y], buffer.at[links.near("y", -steps)])
        for steps in (1, 3, 2)
    ]


def scatter_y(links, outgoing, incoming, partial):
    y = links.y
    outgoing[...] = partial.astype(BF16).reshape(4, ROWS, D)
    waits = [
        links.exchange(
            "y",
            steps,
            outgoing.at[links.near("y", steps)],
            incoming.at[y],
            incoming.at[links.near("y", -steps)],
        )
        for steps in (2, 1, 3)
    ]
    incoming[y] = outgoing[y]
    return waits


def sum_slots(buffer):
    total = buffer[0].astype(F32)
    for slot in range(1, 4):
        total = total + buffer[slot].astype(F32)
    return total


class Gather:
    def __init__(self, links, buffer, layer):
        self.links, self.buffer, self.layer = links, buffer, layer

    def block(self, first, second):
        x, z = self.links.place(first, second)
        return self.buffer.at[self.layer, self.links.section, x, z]

    def begin(self):
        own = self.block(0, 0)
        exchange = self.links.exchange
        self.first = [
            exchange("first", steps, own, own, self.block(-steps, 0)) for steps in (1, 3, 2)
        ]
        self.second = [
            exchange("second", steps, own, own, self.block(0, -steps)) for steps in (1, 3, 2)
        ]

    def forward(self):
        for wait, first in zip(self.first, (1, 3, 2)):
            wait()
            came = self.block(-first, 0)
            for steps in (1, 3, 2):
                self.second.append(
                    self.links.exchange(
                        "second", steps, came, came, self.block(-first, -steps)
                    )
                )

    def cross(self):
        wait_all(self.second)
        s = self.links.section
        mine = self.buffer.at[self.layer, s]
        self.finish = self.links.exchange("s", 1, mine, mine, self.buffer.at[self.layer, 1 - s])


class Scatter:
    def __init__(self, links, layer, grads, crossed, work, arrived, middle, ended, done, other):
        self.links, self.layer, self.grads, self.crossed = links, layer, grads, crossed
        self.work, self.arrived, self.middle, self.ended = work, arrived, middle, ended
        self.done, self.other = done.at[layer], other.at[layer]
        s, x, z = links.section, links.x, links.z
        self.first_index = z * (1 - s) + x * s
        self.second_index = x * (1 - s) + z * s

    def begin(self):
        s = self.links.section
        self.crossing = self.links.exchange(
            "s", 1, self.grads.at[self.layer, 1 - s], self.crossed, self.crossed
        )

    def spread(self, axis, index, source, target):
        waits = []
        for steps in (2, 1, 3):
            waits.append(
                self.links.exchange(
                    axis,
                    steps,
                    source.at[(index + steps) % 4],
                    target.at[index],
                    target.at[(index + 4 - steps) % 4],
                )
            )
        target[index] = source[index]
        return waits

    def first(self):
        self.crossing()
        s = self.links.section

        def add(first, carry):
            for second in range(4):
                x = first * s + second * (1 - s)
                z = first * (1 - s) + second * s
                mine = self.grads[self.layer, s, x, z].astype(F32)
                self.work[first, second] = (mine + self.crossed[x, z].astype(F32)).astype(BF16)
            return carry

        lax.fori_loop(0, 4, add, 0)
        self.waits = self.spread("first", self.first_index, self.work, self.arrived)

    def second(self):
        wait_all(self.waits)
        self.middle[...] = sum_slots(self.arrived).astype(BF16)
        self.waits = self.spread("second", self.second_index, self.middle, self.ended)

    def last(self):
        wait_all(self.waits)
        self.done[...] = sum_slots(self.ended)
        self.finish = self.links.exchange("s", 1, self.done, self.other, self.other)


def kernel(
    inputs,
    cotangent,
    own_wide,
    own_narrow,
    own_params,
    activations,
    input_grads,
    wide_out,
    narrow_out,
    param_grads,
    send_sems,
    recv_sems,
    wide,
    narrow,
    params,
    normed_one,
    normed_two,
    grad_outs,
    grad_branches,
    scatter_out,
    scatter_in,
    pairs,
    scores,
    probs,
    queries,
    totals,
    attended,
    hidden,
    middles,
    actives,
    slopes,
    pair_grads,
    pair_in_a,
    pair_in_b,
    pair_mid_a,
    pair_mid_b,
    pair_end_a,
    pair_end_b,
    wide_grads,
    narrow_grads,
    wide_crossed,
    wide_work,
    wide_arrived,
    wide_middle,
    wide_ended,
    wide_done,
    wide_other,
    narrow_crossed,
    narrow_work,
    narrow_arrived,
    narrow_middle,
    narrow_ended,
    narrow_done,
    narrow_other,
    sums,
    sums_cross,
    sums_y,
    sums_z,
    sums_x,
    outputs,
    output_cross,
    in_grads,
    in_grad_cross,
):
    links = Links(send_sems, recv_sems)
    s, x, z, y, row = links.section, links.x, links.z, links.y, links.row
    other = 1 - s
    wide[s, :, x, z] = own_wide[...]
    narrow[s, :, x, z] = own_narrow[...]
    params[s] = own_params[...]
    links.barrier()

    narrow_wait = links.exchange(
        "s", 1, own_narrow.at[other], narrow.at[s, other, x, z], narrow.at[other, s, x, z]
    )
    params_wait = links.exchange("s", 1, params.at[s], params.at[s], params.at[other])
    wide_wait = links.exchange(
        "s", 1, own_wide.at[other], wide.at[s, other, x, z], wide.at[other, s, x, z]
    )
    narrow_gathers = [Gather(links, narrow, layer) for layer in range(2)]
    wide_gathers = [Gather(links, wide, layer) for layer in range(2)]
    narrow_wait()
    narrow_gathers[0].begin()
    params_wait()

    def norm_rows(layer, current):
        hidden[layer] = current
        normed, _, _ = norm_parts(current, params[layer, 0:1, :], params[layer, 1:2, :])
        normed_one[layer, y] = normed.astype(BF16)
        return gather_y(links, normed_one.at[layer])

    normed_waits = norm_rows(0, inputs[s].astype(F32))

    wide_wait()
    narrow_gathers[0].forward()
    wide_gathers[0].begin()
    narrow_gathers[0].cross()

    def matrix(buffer, layer, half):
        return buffer[layer, half].reshape(D, buffer.shape[-1])

    def part(layer, columns):
        return narrow[layer, 1, :, :, :, columns].reshape(D, 256)

    query_part, out_part = slice(0, 256), slice(128, 384)

    def forward(layer, normed_waits):
        wait_all(normed_waits)
        narrow_gathers[layer].finish()
        normed = normed_one[layer].reshape(FULL, D)
        pair = dot_nn(normed, matrix(narrow, layer, 0)) + params[layer, 7:8, 0:384]
        pairs[layer, x, z] = pair.astype(BF16)
        own = pairs.at[layer]
        low, high = pl.ds(0, 64), pl.ds(64, 64)
        pair_first_a = [
            links.exchange(
                "z",
                steps,
                own.at[x, z, low],
                own.at[x, z, low],
                own.at[x, links.near("z", -steps), low],
            )
            for steps in (1, 3, 2)
        ]
        pair_first_b = [
            links.exchange(
                "x",
                steps,
                own.at[x, z, high],
                own.at[x, z, high],
                own.at[links.near("x", -steps), z, high],
            )
            for steps in (1, 3, 2)
        ]
        query = dot_nn(normed, part(layer, query_part)) + params[layer, 7:8, 384:640]
        query = query.astype(BF16).astype(F32) * 0.125
        queries[layer] = spread_heads(query, 0).astype(BF16)
        wait_all(pair_first_a)
        pair_second_a = [
            links.exchange(
                "x",
                steps,
                own.at[x, :, low],
                own.at[x, :, low],
                own.at[links.near("x", -steps), :, low],
            )
            for steps in (1, 3, 2)
        ]
        wait_all(pair_first_b)
        pair_second_b = [
            links.exchange(
                "z",
                steps,
                own.at[:, z, high],
                own.at[:, z, high],
                own.at[:, links.near("z", -steps), high],
            )
            for steps in (1, 3, 2)
        ]
        if layer == 0:
            wide_gathers[0].forward()
        else:
            wide_gathers[1].cross()
        wait_all(pair_second_a)
        wait_all(pair_second_b)

        stacked = queries[layer]
        position = lax.broadcasted_iota(jnp.int32, (STACK, CHUNK), 0) % FULL + row * FULL
        column = lax.broadcasted_iota(jnp.int32, (STACK, CHUNK), 1)

        def find_top(chunk, running):
            keys = pairs[layer, chunk, :, :, 0:256].reshape(CHUNK, 256)
            raw = dot_nt(stacked, keys)
            raw = jnp.where(column + chunk * CHUNK <= position, raw, MASKED)
            scores[chunk] = raw
            return jnp.maximum(running, jnp.max(raw, axis=1, keepdims=True))

        top = lax.fori_loop(0, x + 1, find_top, jnp.full((STACK, 1), MASKED, F32))

        def add_chunk(chunk, carry):
            total, summed = carry
            weight = jnp.exp(scores[chunk] - top)
            rounded = weight.astype(BF16)
            probs[layer, chunk] = rounded
            values = pairs[layer, chunk, :, :, 128:384].reshape(CHUNK, 256)
            return (
                total + jnp.sum(weight, axis=1, keepdims=True),
                summed + dot_nn(rounded, values),
            )

        total, summed = lax.fori_loop(
            0, x + 1, add_chunk, (jnp.zeros((STACK, 1), F32), jnp.zeros((STACK, 256), F32))
        )
        totals[layer] = total
        attention = join_heads(summed / total, HD)
        attended[layer] = attention
        partial = dot_nt(attention.astype(BF16), part(layer, out_part))
        waits = scatter_y(links, scatter_out.at[layer, 0], scatter_in.at[layer, 0], partial)
        if layer == 0:
            wide_gathers[0].cross()
            narrow_gathers[1].begin()
            wide_gathers[1].begin()
        wait_all(waits)
        middle = hidden[layer] + sum_slots(scatter_in.at[layer, 0]) + params[layer, 2:3, :]
        middles[layer] = middle
        second, _, _ = norm_parts(middle, params[layer, 3:4, :], params[layer, 4:5, :])
        normed_two[layer, y] = second.astype(BF16)
        waits = gather_y(links, normed_two.at[layer])
        if layer == 0:
            narrow_gathers[1].forward()
            wide_gathers[1].forward()
        wait_all(waits)
        wide_gathers[layer].finish()
        upward = (
            dot_nn(normed_two[layer].reshape(FULL, D), matrix(wide, layer, 0)) + params[layer, 6:7, :]
        )
        active, slope = gelu_parts(upward)
        actives[layer] = active.astype(BF16)
        slopes[layer] = slope
        partial = dot_nt(actives[layer], matrix(wide, layer, 1))
        waits = scatter_y(links, scatter_out.at[layer, 1], scatter_in.at[layer, 1], partial)
        if layer == 0:
            narrow_gathers[1].cross()
        wait_all(waits)
        result = middle + sum_slots(scatter_in.at[layer, 1]) + params[layer, 5:6, :]
        outputs[layer] = result.astype(BF16)

    forward(0, normed_waits)
    forward(1, norm_rows(1, outputs[0].astype(F32)))
    output_wait = links.exchange("s", 1, outputs.at[other], output_cross, output_cross)

    def scatters(layer):
        wide_scatter = Scatter(
            links,
            layer,
            wide_grads,
            wide_crossed.at[layer],
            wide_work.at[layer],
            wide_arrived.at[layer],
            wide_middle.at[layer],
            wide_ended.at[layer],
            wide_done,
            wide_other,
        )
        narrow_scatter = Scatter(
            links,
            layer,
            narrow_grads,
            narrow_crossed.at[layer],
            narrow_work.at[layer],
            narrow_arrived.at[layer],
            narrow_middle.at[layer],
            narrow_ended.at[layer],
            narrow_done,
            narrow_other,
        )
        return wide_scatter, narrow_scatter

    wide_scatters, narrow_scatters = zip(scatters(0), scatters(1))

    def backward(layer, grad_rows):
        grad_outs[layer, y] = grad_rows
        waits = gather_y(links, grad_outs.at[layer])
        sums[layer, 5:6, :] = column_sum(grad_rows.astype(F32))
        gain_one, gain_two = params[layer, 0:1, :], params[layer, 3:4, :]
        _, unit_one, factor_one = norm_parts(hidden[layer], gain_one, gain_one)
        _, unit_two, factor_two = norm_parts(middles[layer], gain_two, gain_two)
        if layer == 0:
            narrow_scatters[1].first()
        wait_all(waits)
        grad_full = grad_outs[layer].reshape(FULL, D)
        grad_up = (dot_nn(grad_full, matrix(wide, layer, 1)) * slopes[layer]).astype(BF16)
        partial = dot_nt(grad_up, matrix(wide, layer, 0))
        waits = scatter_y(links, scatter_out.at[layer, 2], scatter_in.at[layer, 2], partial)
        down_grad = dot_tn(grad_full, actives[layer])
        wide_grads[layer, 1] = down_grad.astype(BF16).reshape(4, 4, SHARD, WIDE)
        up_grad = dot_tn(normed_two[layer].reshape(FULL, D), grad_up)
        wide_grads[layer, 0] = up_grad.astype(BF16).reshape(4, 4, SHARD, WIDE)
        wide_scatters[layer].begin()
        if layer == 0:
            narrow_scatters[1].second()
        sums[layer, 6:7, :] = column_sum(grad_up.astype(F32))
        wait_all(waits)
        grad_two = sum_slots(scatter_in.at[layer, 2])
        grad_middle = grad_rows.astype(F32) + norm_back(grad_two, unit_two, factor_two, gain_two)
        grad_branches[layer, y] = grad_middle.astype(BF16)
        waits = gather_y(links, grad_branches.at[layer])
        sums[layer, 2:3, :] = column_sum(grad_middle)
        sums[layer, 3:4, :] = column_sum(grad_two * unit_two)
        sums[layer, 4:5, :] = column_sum(grad_two)
        wide_scatters[layer].first()
        wait_all(waits)
        branch_full = grad_branches[layer].reshape(FULL, D)
        grad_mixed = dot_nn(branch_full, part(layer, out_part)).astype(BF16).astype(F32)
        stacked_grad = spread_heads(grad_mixed, HD)
        delta = jnp.sum(spread_heads(grad_mixed * attended[layer], HD), axis=1, keepdims=True)
        inverse = 1.0 / totals[layer]
        scaled_grad = (stacked_grad * inverse).astype(BF16)
        stacked_grad = stacked_grad.astype(BF16)
        stacked = queries[layer]

        def chunk_back(chunk, summed):
            keys = pairs[layer, chunk, :, :, 0:256].reshape(CHUNK, 256)
            values = pairs[layer, chunk, :, :, 128:384].reshape(CHUNK, 256)
            weight = probs[layer, chunk]
            products = dot_nt(stacked_grad, values)
            score_grad = (weight.astype(F32) * (products - delta) * inverse).astype(BF16)
            key_grad = dot_tn(score_grad, stacked)
            value_grad = dot_tn(weight, scaled_grad)
            joined = jnp.concatenate(
                [
                    key_grad[:, :128],
                    key_grad[:, 128:] + value_grad[:, :128],
                    value_grad[:, 128:],
                ],
                axis=1,
            )
            pair_grads[layer, chunk] = joined.astype(BF16).reshape(4, FULL, 384)
            return summed + dot_nn(score_grad, keys)

        def chunk_clear(chunk, carry):
            pair_grads[layer, chunk] = jnp.zeros((4, FULL, 384), BF16)
            return carry

        lax.fori_loop(x + 1, 4, chunk_clear, 0)
        query_sum = lax.fori_loop(0, x + 1, chunk_back, jnp.zeros((STACK, 256), F32))
        own = pair_grads.at[layer]
        low, high = pl.ds(0, 64), pl.ds(64, 64)
        waits_a = [
            links.exchange(
                "x",
                steps,
                own.at[links.near("x", steps), :, low],
                pair_in_a.at[layer, x],
                pair_in_a.at[layer, links.near("x", -steps)],
            )
            for steps in (2, 1, 3)
        ]
        waits_b = [
            links.exchange(
                "z",
                steps,
                own.at[:, links.near("z", steps), high],
                pair_in_b.at[layer, z],
                pair_in_b.at[layer, links.near("z", -steps)],
            )
            for steps in (2, 1, 3)
        ]
        pair_in_a[layer, x] = pair_grads[layer, x, :, 0:64]
        pair_in_b[layer, z] = pair_grads[layer, :, z, 64:128]
        grad_query = (join_heads(query_sum, 0) * 0.125).astype(BF16)
        normed = normed_one[layer].reshape(FULL, D)
        query_grad = dot_tn(normed, grad_query)
        out_grad = dot_tn(branch_full, attended[layer].astype(BF16))
        joined = jnp.concatenate(
            [
                query_grad[:, :128],
                query_grad[:, 128:] + out_grad[:, :128],
                out_grad[:, 128:],
            ],
            axis=1,
        )
        narrow_grads[layer, 1] = joined.astype(BF16).reshape(4, 4, SHARD, NARROW)
        partial = dot_nt(grad_query, part(layer, query_part))
        wide_scatters[layer].second()
        if layer == 0:
            narrow_scatters[1].last()
        wait_all(waits_a)
        pair_mid_a[layer] = sum_slots(pair_in_a.at[layer]).astype(BF16)
        waits_a = [
            links.exchange(
                "z",
                steps,
                pair_mid_a.at[layer, links.near("z", steps)],
                pair_end_a.at[layer, z],
                pair_end_a.at[layer, links.near("z", -steps)],
            )
            for steps in (2, 1, 3)
        ]
        pair_end_a[layer, z] = pair_mid_a[layer, z]
        wait_all(waits_b)
        pair_mid_b[layer] = sum_slots(pair_in_b.at[layer]).astype(BF16)
        waits_b = [
            links.exchange(
                "x",
                steps,
                pair_mid_b.at[layer, links.near("x", steps)],
                pair_end_b.at[layer, x],
                pair_end_b.at[layer, links.near("x", -steps)],
            )
            for steps in (2, 1, 3)
        ]
        pair_end_b[layer, x] = pair_mid_b[layer, x]
        wait_all(waits_a)
        wait_all(waits_b)
        grad_pair = jnp.concatenate(
            [sum_slots(pair_end_a.at[layer]), sum_slots(pair_end_b.at[layer])], axis=0
        ).astype(BF16)
        partial = partial + dot_nt(grad_pair, matrix(narrow, layer, 0))
        waits = scatter_y(links, scatter_out.at[layer, 3], scatter_in.at[layer, 3], partial)
        pair_weight_grad = dot_tn(normed, grad_pair)
        narrow_grads[layer, 0] = pair_weight_grad.astype(BF16).reshape(4, 4, SHARD, NARROW)
        narrow_scatters[layer].begin()
        wide_scatters[layer].last()
        sums[layer, 7:8, :] = jnp.concatenate(
            [
                column_sum(grad_pair.astype(F32)),
                column_sum(grad_query.astype(F32)),
                jnp.zeros((1, 128), F32),
            ],
            axis=1,
        )
        wait_all(waits)
        grad_one = sum_slots(scatter_in.at[layer, 3])
        sums[layer, 0:1, :] = column_sum(grad_one * unit_one)
        sums[layer, 1:2, :] = column_sum(grad_one)
        grad_input = grad_middle + norm_back(grad_one, unit_one, factor_one, gain_one)
        in_grads[layer] = grad_input.astype(BF16)

    backward(1, cotangent[s])
    backward(0, in_grads[1])
    in_grad_wait = links.exchange("s", 1, in_grads.at[other], in_grad_cross, in_grad_cross)

    sums_wait = links.exchange("s", 1, sums.at[other], sums_cross, sums_cross)
    narrow_scatters[0].first()
    sums_wait()
    sums_y[y] = sums[s] + sums_cross[...]
    waits = gather_y(links, sums_y)
    output_wait()
    activations[s] = outputs[s]
    activations[other] = output_cross[...]
    wait_all(waits)
    sums_z[z] = jnp.concatenate([sum_slots(sums_y)[0:6], sums_y[y, 6:8, :]], axis=0)
    waits = [
        links.exchange(
            "z", steps, sums_z.at[z], sums_z.at[z], sums_z.at[links.near("z", -steps)]
        )
        for steps in (1, 3, 2)
    ]
    narrow_scatters[0].second()
    in_grad_wait()
    input_grads[s] = in_grads[s]
    input_grads[other] = in_grad_cross[...]
    wait_all(waits)
    sums_x[x] = sum_slots(sums_z)
    waits = [
        links.exchange(
            "x", steps, sums_x.at[x], sums_x.at[x], sums_x.at[links.near("x", -steps)]
        )
        for steps in (1, 3, 2)
    ]
    narrow_scatters[0].last()
    wait_all(waits)
    param_grads[...] = sum_slots(sums_x)
    for layer in range(2):
        wide_scatters[layer].finish()
        narrow_scatters[layer].finish()
    wide_out[s] = wide_done[s]
    wide_out[other] = wide_other[s]
    narrow_out[s] = narrow_done[s]
    narrow_out[other] = narrow_other[s]
    links.finish()


def scratch_shapes():
    def low(*shape):
        return pltpu.VMEM(shape, BF16)

    def full(*shape):
        return pltpu.VMEM(shape, F32)

    return [
        pltpu.SemaphoreType.DMA((SEMS,)),
        pltpu.SemaphoreType.DMA((SEMS,)),
        low(2, 2, 4, 4, SHARD, WIDE),
        low(2, 2, 4, 4, SHARD, NARROW),
        full(2, 8, D),
        low(2, 4, ROWS, D),
        low(2, 4, ROWS, D),
        low(2, 4, ROWS, D),
        low(2, 4, ROWS, D),
        low(2, 4, 4, ROWS, D),
        low(2, 4, 4, ROWS, D),
        low(2, 4, 4, FULL, 384),
        full(4, STACK, CHUNK),
        low(2, 4, STACK, CHUNK),
        low(2, STACK, 256),
        full(2, STACK, 1),
        full(2, FULL, 256),
        full(2, ROWS, D),
        full(2, ROWS, D),
        low(2, FULL, D),
        full(2, FULL, D),
        low(2, 4, 4, FULL, 384),
        low(2, 4, 4, 64, 384),
        low(2, 4, 4, 64, 384),
        low(2, 4, 64, 384),
        low(2, 4, 64, 384),
        low(2, 4, 64, 384),
        low(2, 4, 64, 384),
        low(2, 2, 4, 4, SHARD, WIDE),
        low(2, 2, 4, 4, SHARD, NARROW),
        low(2, 4, 4, SHARD, WIDE),
        low(2, 4, 4, SHARD, WIDE),
        low(2, 4, 4, SHARD, WIDE),
        low(2, 4, SHARD, WIDE),
        low(2, 4, SHARD, WIDE),
        full(2, SHARD, WIDE),
        full(2, SHARD, WIDE),
        low(2, 4, 4, SHARD, NARROW),
        low(2, 4, 4, SHARD, NARROW),
        low(2, 4, 4, SHARD, NARROW),
        low(2, 4, SHARD, NARROW),
        low(2, 4, SHARD, NARROW),
        full(2, SHARD, NARROW),
        full(2, SHARD, NARROW),
        full(2, 8, D),
        full(8, D),
        full(4, 8, D),
        full(4, 8, D),
        full(4, 8, D),
        low(2, ROWS, D),
        low(ROWS, D),
        low(2, ROWS, D),
        low(ROWS, D),
    ]


def local(
    inputs,
    cotangent,
    ln1_gain,
    ln1_bias,
    w_qkv,
    b_qv,
    w_out,
    b_out,
    ln2_gain,
    ln2_bias,
    w_up,
    b_up,
    w_down,
    b_down,
):
    wide = jnp.stack([w_up[0], w_down[0].T])
    narrow = jnp.stack(
        [
            jnp.concatenate([w_qkv[0, :, 1], w_qkv[0, :, 2]], axis=1),
            jnp.concatenate([w_qkv[0, :, 0], w_out[0].T], axis=1),
        ]
    )
    biases = jnp.concatenate(
        [jnp.zeros((1, 192), F32), b_qv[:, 1], b_qv[:, 0], jnp.zeros((1, 192), F32)], axis=1
    )
    params = jnp.concatenate(
        [ln1_gain, ln1_bias, b_out, ln2_gain, ln2_bias, b_down, b_up, biases], axis=0
    )
    whole = pl.BlockSpec(memory_space=pltpu.VMEM)
    acts, in_grads, wide_grads, narrow_grads, sums = pl.pallas_call(
        kernel,
        name="layers",
        out_shape=(
            jax.ShapeDtypeStruct((2, ROWS, D), BF16),
            jax.ShapeDtypeStruct((2, ROWS, D), BF16),
            jax.ShapeDtypeStruct((2, SHARD, WIDE), F32),
            jax.ShapeDtypeStruct((2, SHARD, NARROW), F32),
            jax.ShapeDtypeStruct((8, D), F32),
        ),
        in_specs=[whole] * 5,
        out_specs=(whole,) * 5,
        scratch_shapes=scratch_shapes(),
        compiler_params=pltpu.CompilerParams(
            collective_id=0, has_side_effects=True, vmem_limit_bytes=60 * 2**20
        ),
    )(inputs, cotangent, wide, narrow, params)
    qkv_grad = jnp.stack(
        [narrow_grads[1, :, :192], narrow_grads[0, :, :192], narrow_grads[0, :, 192:]],
        axis=1,
    )
    return (
        acts[None],
        in_grads[None],
        sums[0:1],
        sums[1:2],
        qkv_grad[None],
        jnp.stack([sums[7, 384:576], sums[7, 192:384]])[None],
        narrow_grads[1, :, 192:].T[None],
        sums[2:3],
        sums[3:4],
        sums[4:5],
        wide_grads[0][None],
        sums[6:7],
        wide_grads[1].T[None],
        sums[5:6],
    )


def solution(mesh):
    rows = P(None, ("gx", "gy"), None)
    vector = P("section", None)
    qkv = P("section", "gx", None, "gy")
    bias_qv = P("section", None, "gy")
    out = P("section", "gy", "gx")
    up = P("section", "gx", "gy")
    hidden = P("section", "gy")
    sharded = (vector, vector, qkv, bias_qv, out, vector, vector, vector, up, hidden, out, vector)
    layer_rows = P("section", None, ("gx", "gy"), None)
    return jax.shard_map(
        local,
        mesh=mesh,
        in_specs=(rows, rows) + sharded,
        out_specs=(layer_rows, layer_rows) + sharded,
        check_vma=False,
    )
```

```python
import jax
import jax.numpy as jnp
from jax import lax
from jax.experimental import pallas as pl
from jax.experimental.pallas import tpu as pltpu
from jax.sharding import PartitionSpec as P

HD = 64
EPSILON = 1e-05
MASKED = -1e30
MESH = pl.DeviceIdType.MESH
F32 = jnp.float32
BF16 = jnp.bfloat16

ROWS = 32
FULL = 128
D = 768
CHUNK = 512
HEADS = 3
STACK = HEADS * FULL

WIDE = 768
NARROW = 384
SHARD = 48
SEMS = 240


def dot_nn(a, b):
    return lax.dot_general(a, b, (((1,), (0,)), ((), ())), preferred_element_type=F32)


def dot_nt(a, b):
    return lax.dot_general(a, b, (((1,), (1,)), ((), ())), preferred_element_type=F32)


def dot_tn(a, b):
    return lax.dot_general(a, b, (((0,), (0,)), ((), ())), preferred_element_type=F32)


def norm_parts(values, gain, offset):
    average = jnp.mean(values, axis=-1, keepdims=True)
    centered = values - average
    variance = jnp.mean(centered * centered, axis=-1, keepdims=True)
    factor = lax.rsqrt(variance + EPSILON)
    unit_rows = centered * factor
    return (unit_rows * gain + offset, unit_rows, factor)


def norm_back(grad_rows, unit_rows, factor, gain):
    scaled = grad_rows * gain
    first_mean = jnp.mean(scaled, axis=-1, keepdims=True)
    second_mean = jnp.mean(scaled * unit_rows, axis=-1, keepdims=True)
    return factor * (scaled - first_mean - unit_rows * second_mean)


def gelu_parts(values):
    scale = 0.7978845608028654
    inner = scale * (values + 0.044715 * values * values * values)
    bent = jnp.tanh(inner)
    active = 0.5 * values * (1.0 + bent)
    slope = 0.5 * (1.0 + bent) + 0.5 * values * (1.0 - bent * bent) * scale * (
        1.0 + 3.0 * 0.044715 * values * values
    )
    return active, slope


def column_sum(values):
    return jnp.sum(values, axis=0, keepdims=True)


def head_mask(head, first):
    lane = lax.broadcasted_iota(jnp.int32, (FULL, 256), 1)
    low = first + HD * head
    return jnp.logical_and(lane >= low, lane < low + HD)


def spread_heads(values, first):
    return jnp.concatenate(
        [jnp.where(head_mask(head, first), values, 0.0) for head in range(HEADS)], axis=0
    )


def join_heads(stacked, first):
    total = jnp.zeros((FULL, 256), F32)
    for head in range(HEADS):
        part = stacked[head * FULL : (head + 1) * FULL]
        total = total + jnp.where(head_mask(head, first), part, 0.0)
    return total


class Links:
    def __init__(self, send_sems, recv_sems):
        self.send_sems, self.recv_sems = send_sems, recv_sems
        self.count = 0
        self.sent = []
        self.section = lax.axis_index("section")
        self.row = lax.axis_index("gx")
        self.y = lax.axis_index("gy")
        self.x = self.row // 4
        self.z = self.row % 4

    def near(self, axis, steps):
        if axis == "s":
            return 1 - self.section
        return (getattr(self, axis) + (steps + 4)) % 4

    def place(self, first, second):
        s = self.section
        x = (self.x + (first + 4) * s + (second + 4) * (1 - s)) % 4
        z = (self.z + (first + 4) * (1 - s) + (second + 4) * s) % 4
        return x, z

    def device(self, axis, steps):
        s, x, z, y = self.section, self.x, self.z, self.y
        if axis == "first":
            x, z = self.place(steps, 0)
            return (s, x * 4 + z, y)
        if axis == "second":
            x, z = self.place(0, steps)
            return (s, x * 4 + z, y)
        there = self.near(axis, steps)
        if axis == "s":
            s = there
        elif axis == "x":
            x = there
        elif axis == "z":
            z = there
        else:
            y = there
        return (s, x * 4 + z, y)

    def exchange(self, axis, steps, source, target, landing):
        index = self.count
        self.count += 1
        sems = (self.send_sems.at[index], self.recv_sems.at[index])
        copy = pltpu.make_async_remote_copy(
            source, target, *sems, device_id=self.device(axis, steps), device_id_type=MESH
        )
        copy.start()
        self.sent.append(copy)
        arrival = pltpu.make_async_remote_copy(
            landing, landing, *sems, device_id=self.device(axis, -steps), device_id_type=MESH
        )
        return arrival.wait_recv

    def barrier(self):
        barrier = pltpu.get_barrier_semaphore()
        peers = [("s", 1)] + [(axis, steps) for axis in "xyz" for steps in (1, 2, 3)]
        for axis, steps in peers:
            pl.semaphore_signal(
                barrier, inc=1, device_id=self.device(axis, steps), device_id_type=MESH
            )
        pl.semaphore_wait(barrier, len(peers))

    def finish(self):
        for copy in self.sent:
            copy.wait_send()
        self.sent = []


def wait_all(waits):
    for wait in waits:
        wait()


def gather_y(links, buffer):
    y = links.y
    return [
        links.exchange("y", steps, buffer.at[y], buffer.at[y], buffer.at[links.near("y", -steps)])
        for steps in (1, 3, 2)
    ]


def scatter_y(links, outgoing, incoming, partial):
    y = links.y
    outgoing[...] = partial.astype(BF16).reshape(4, ROWS, D)
    waits = [
        links.exchange(
            "y",
            steps,
            outgoing.at[links.near("y", steps)],
            incoming.at[y],
            incoming.at[links.near("y", -steps)],
        )
        for steps in (2, 1, 3)
    ]
    incoming[y] = outgoing[y]
    return waits


def sum_slots(buffer):
    total = buffer[0].astype(F32)
    for slot in range(1, 4):
        total = total + buffer[slot].astype(F32)
    return total


SCHEDULE = {
    "f0_q": ("w0.begin", "w0.own"),
    "f0_kv": ("w0.forward",),
    "f0_rs1": ("w0.relay", "w0.cross", "n1.begin", "n1.own"),
    "f0_ag2": ("n1.forward", "w1.begin", "w1.own"),
    "f0_rs2": ("n1.relay", "n1.cross", "w1.forward"),
    "f1_kv": ("w1.relay",),
    "f1_rs1": ("w1.cross",),
    "b1_rs1": ("W1.begin",),
    "b1_ag2": ("W1.first",),
    "b1_kv1": ("W1.second",),
    "b1_rs2": ("N1.begin", "W1.last"),
    "b0_ag": ("N1.first",),
    "b0_rs1": ("W0.begin", "N1.second"),
    "b0_ag2": ("W0.first",),
    "b0_kv1": ("W0.second", "N1.last"),
    "b0_rs2": ("N0.begin", "W0.last"),
}
RELAYED = ()


class Gather:
    def __init__(self, links, buffer, layer, relayed):
        self.links, self.buffer, self.layer = links, buffer, layer
        self.relayed = relayed
        self.near = []
        self.far = []

    def block(self, first, second):
        x, z = self.links.place(first, second)
        return self.buffer.at[self.layer, self.links.section, x, z]

    def begin(self):
        own = self.block(0, 0)
        self.first = [
            self.links.exchange("first", steps, own, own, self.block(-steps, 0))
            for steps in (1, 3, 2)
        ]

    def send(self, first):
        came = self.block(-first, 0)
        for steps in (1, 3) if self.relayed else (1, 3, 2):
            wait = self.links.exchange("second", steps, came, came, self.block(-first, -steps))
            (self.near if steps != 2 else self.far).append(wait)

    def own(self):
        self.send(0)

    def forward(self):
        for wait, first in zip(self.first, (1, 3, 2)):
            wait()
            self.send(first)

    def relay(self):
        wait_all(self.near)
        self.near = []
        if self.relayed:
            for first, steps in zip((0, 1, 3, 2), (1, 3, 1, 3)):
                came = self.block(-first, -steps)
                self.far.append(
                    self.links.exchange("second", steps, came, came, self.block(-first, -2))
                )

    def cross(self):
        wait_all(self.near + self.far)
        s = self.links.section
        mine = self.buffer.at[self.layer, s]
        self.finish = self.links.exchange("s", 1, mine, mine, self.buffer.at[self.layer, 1 - s])


class Scatter:
    def __init__(self, links, layer, grads, crossed, work, arrived, middle, ended, done, other):
        self.links, self.layer, self.grads, self.crossed = links, layer, grads, crossed
        self.work, self.arrived, self.middle, self.ended = work, arrived, middle, ended
        self.done, self.other = done.at[layer], other.at[layer]
        s, x, z = links.section, links.x, links.z
        self.first_index = z * (1 - s) + x * s
        self.second_index = x * (1 - s) + z * s

    def begin(self):
        s = self.links.section
        self.crossing = self.links.exchange(
            "s", 1, self.grads.at[self.layer, 1 - s], self.crossed, self.crossed
        )

    def spread(self, axis, index, source, target):
        waits = []
        for steps in (2, 1, 3):
            waits.append(
                self.links.exchange(
                    axis,
                    steps,
                    source.at[(index + steps) % 4],
                    target.at[index],
                    target.at[(index + 4 - steps) % 4],
                )
            )
        target[index] = source[index]
        return waits

    def first(self):
        self.crossing()
        s = self.links.section

        def add(first, carry):
            for second in range(4):
                x = first * s + second * (1 - s)
                z = first * (1 - s) + second * s
                mine = self.grads[self.layer, s, x, z].astype(F32)
                self.work[first, second] = (mine + self.crossed[x, z].astype(F32)).astype(BF16)
            return carry

        lax.fori_loop(0, 4, add, 0)
        self.waits = self.spread("first", self.first_index, self.work, self.arrived)

    def second(self):
        wait_all(self.waits)
        self.middle[...] = sum_slots(self.arrived).astype(BF16)
        self.waits = self.spread("second", self.second_index, self.middle, self.ended)

    def last(self):
        wait_all(self.waits)
        self.done[...] = sum_slots(self.ended)
        self.finish = self.links.exchange("s", 1, self.done, self.other, self.other)


def kernel(
    inputs,
    cotangent,
    ln1_gain,
    ln1_bias,
    w_qkv,
    b_qv,
    w_out,
    b_out,
    ln2_gain,
    ln2_bias,
    w_up,
    b_up,
    w_down,
    b_down,
    activations,
    input_grads,
    wide_out,
    narrow_out,
    param_grads,
    send_sems,
    recv_sems,
    own_wide,
    own_narrow,
    wide,
    narrow,
    params,
    normed_one,
    normed_two,
    grad_outs,
    grad_branches,
    scatter_out,
    scatter_in,
    pairs,
    scores,
    probs,
    queries,
    totals,
    attended,
    hidden,
    middles,
    actives,
    slopes,
    pair_grads,
    pair_in_a,
    pair_in_b,
    pair_mid_a,
    pair_mid_b,
    pair_end_a,
    pair_end_b,
    wide_grads,
    narrow_grads,
    wide_crossed,
    wide_work,
    wide_arrived,
    wide_middle,
    wide_ended,
    wide_done,
    wide_other,
    narrow_crossed,
    narrow_work,
    narrow_arrived,
    narrow_middle,
    narrow_ended,
    narrow_done,
    narrow_other,
    sums,
    sums_cross,
    sums_y,
    sums_z,
    sums_x,
    outputs,
    output_cross,
    in_grads,
    in_grad_cross,
):
    links = Links(send_sems, recv_sems)
    s, x, z, y, row = links.section, links.x, links.z, links.y, links.row
    other = 1 - s
    own_wide[0] = w_up[0]
    own_wide[1] = w_down[0]
    own_narrow[0] = jnp.concatenate([w_qkv[0, 1], w_qkv[0, 2]], axis=1)
    own_narrow[1] = jnp.concatenate([w_qkv[0, 0], w_out[0]], axis=1)
    rows = (ln1_gain, ln1_bias, b_out, ln2_gain, ln2_bias, b_down, b_up)
    for index, values in enumerate(rows):
        params[s, index : index + 1, :] = values[...]
    blank = jnp.zeros((1, 192), F32)
    params[s, 7:8, :] = jnp.concatenate([blank, b_qv[0, 1:2], b_qv[0, 0:1], blank], axis=1)
    wide[s, :, x, z] = own_wide[...]
    narrow[s, :, x, z] = own_narrow[...]
    links.barrier()

    narrow_wait = links.exchange(
        "s", 1, own_narrow.at[other], narrow.at[s, other, x, z], narrow.at[other, s, x, z]
    )
    params_wait = links.exchange("s", 1, params.at[s], params.at[s], params.at[other])
    wide_wait = links.exchange(
        "s", 1, own_wide.at[other], wide.at[s, other, x, z], wide.at[other, s, x, z]
    )
    tasks = {}
    for layer in range(2):
        for name, buffer in (("n", narrow), ("w", wide)):
            name = name + str(layer)
            tasks[name] = Gather(links, buffer, layer, name in RELAYED)

    def slot(name):
        for step in SCHEDULE.get(name, ()):
            task, action = step.split(".")
            getattr(tasks[task], action)()

    narrow_wait()
    tasks["n0"].begin()
    tasks["n0"].own()
    params_wait()

    def norm_rows(layer, current):
        hidden[layer] = current
        normed, _, _ = norm_parts(current, params[layer, 0:1, :], params[layer, 1:2, :])
        normed_one[layer, y] = normed.astype(BF16)
        waits = gather_y(links, normed_one.at[layer])
        slot(f"f{layer}_ag")
        return waits

    normed_waits = norm_rows(0, inputs[s].astype(F32))

    wide_wait()
    tasks["n0"].forward()
    slot("w")
    tasks["n0"].relay()
    tasks["n0"].cross()

    def matrix(buffer, layer, half):
        return buffer[layer, half].reshape(D, buffer.shape[-1])

    def part(layer, columns):
        return narrow[layer, 1, :, :, :, columns].reshape(D, 256)

    query_part, out_part = slice(0, 256), slice(128, 384)

    def gather_grads(layer, grad_rows):
        grad_outs[layer, y] = grad_rows
        return gather_y(links, grad_outs.at[layer])

    def forward(layer, normed_waits):
        wait_all(normed_waits)
        tasks[f"n{layer}"].finish()
        normed = normed_one[layer].reshape(FULL, D)
        pair = dot_nn(normed, matrix(narrow, layer, 0)) + params[layer, 7:8, 0:384]
        pairs[layer, x, z] = pair.astype(BF16)
        own = pairs.at[layer]
        low, high = pl.ds(0, 64), pl.ds(64, 64)
        pair_first_a = [
            links.exchange(
                "z",
                steps,
                own.at[x, z, low],
                own.at[x, z, low],
                own.at[x, links.near("z", -steps), low],
            )
            for steps in (1, 3, 2)
        ]
        pair_first_b = [
            links.exchange(
                "x",
                steps,
                own.at[x, z, high],
                own.at[x, z, high],
                own.at[links.near("x", -steps), z, high],
            )
            for steps in (1, 3, 2)
        ]
        query = dot_nn(normed, part(layer, query_part)) + params[layer, 7:8, 384:640]
        query = query.astype(BF16).astype(F32) * 0.125
        queries[layer] = spread_heads(query, 0).astype(BF16)
        slot(f"f{layer}_q")
        wait_all(pair_first_a)
        pair_second_a = [
            links.exchange(
                "x",
                steps,
                own.at[x, :, low],
                own.at[x, :, low],
                own.at[links.near("x", -steps), :, low],
            )
            for steps in (1, 3, 2)
        ]
        wait_all(pair_first_b)
        pair_second_b = [
            links.exchange(
                "z",
                steps,
                own.at[:, z, high],
                own.at[:, z, high],
                own.at[:, links.near("z", -steps), high],
            )
            for steps in (1, 3, 2)
        ]
        slot(f"f{layer}_kv")
        wait_all(pair_second_a)
        wait_all(pair_second_b)

        stacked = queries[layer]
        position = lax.broadcasted_iota(jnp.int32, (STACK, CHUNK), 0) % FULL + row * FULL
        column = lax.broadcasted_iota(jnp.int32, (STACK, CHUNK), 1)

        def find_top(chunk, running):
            keys = pairs[layer, chunk, :, :, 0:256].reshape(CHUNK, 256)
            raw = dot_nt(stacked, keys)
            raw = jnp.where(column + chunk * CHUNK <= position, raw, MASKED)
            scores[chunk] = raw
            return jnp.maximum(running, jnp.max(raw, axis=1, keepdims=True))

        top = lax.fori_loop(0, x + 1, find_top, jnp.full((STACK, 1), MASKED, F32))

        def add_chunk(chunk, carry):
            total, summed = carry
            weight = jnp.exp(scores[chunk] - top)
            rounded = weight.astype(BF16)
            probs[layer, chunk] = rounded
            values = pairs[layer, chunk, :, :, 128:384].reshape(CHUNK, 256)
            return (
                total + jnp.sum(weight, axis=1, keepdims=True),
                summed + dot_nn(rounded, values),
            )

        total, summed = lax.fori_loop(
            0, x + 1, add_chunk, (jnp.zeros((STACK, 1), F32), jnp.zeros((STACK, 256), F32))
        )
        totals[layer] = total
        attention = join_heads(summed / total, HD)
        attended[layer] = attention
        partial = dot_nt(attention.astype(BF16), part(layer, out_part))
        waits = scatter_y(links, scatter_out.at[layer, 0], scatter_in.at[layer, 0], partial)
        slot(f"f{layer}_rs1")
        wait_all(waits)
        middle = hidden[layer] + sum_slots(scatter_in.at[layer, 0]) + params[layer, 2:3, :]
        middles[layer] = middle
        second, _, _ = norm_parts(middle, params[layer, 3:4, :], params[layer, 4:5, :])
        normed_two[layer, y] = second.astype(BF16)
        waits = gather_y(links, normed_two.at[layer])
        slot(f"f{layer}_ag2")
        wait_all(waits)
        tasks[f"w{layer}"].finish()
        upward = (
            dot_nn(normed_two[layer].reshape(FULL, D), matrix(wide, layer, 0)) + params[layer, 6:7, :]
        )
        active, slope = gelu_parts(upward)
        actives[layer] = active.astype(BF16)
        slopes[layer] = slope
        partial = dot_nt(actives[layer], matrix(wide, layer, 1))
        waits = scatter_y(links, scatter_out.at[layer, 1], scatter_in.at[layer, 1], partial)
        slot(f"f{layer}_rs2")
        wait_all(waits)
        result = middle + sum_slots(scatter_in.at[layer, 1]) + params[layer, 5:6, :]
        outputs[layer] = result.astype(BF16)

    forward(0, normed_waits)
    cotangent_waits = gather_grads(1, cotangent[s])
    forward(1, norm_rows(1, outputs[0].astype(F32)))
    output_wait = links.exchange("s", 1, outputs.at[other], output_cross, output_cross)

    def scatters(layer):
        wide_scatter = Scatter(
            links,
            layer,
            wide_grads,
            wide_crossed.at[layer],
            wide_work.at[layer],
            wide_arrived.at[layer],
            wide_middle.at[layer],
            wide_ended.at[layer],
            wide_done,
            wide_other,
        )
        narrow_scatter = Scatter(
            links,
            layer,
            narrow_grads,
            narrow_crossed.at[layer],
            narrow_work.at[layer],
            narrow_arrived.at[layer],
            narrow_middle.at[layer],
            narrow_ended.at[layer],
            narrow_done,
            narrow_other,
        )
        return wide_scatter, narrow_scatter

    for layer in range(2):
        tasks[f"W{layer}"], tasks[f"N{layer}"] = scatters(layer)

    def backward(layer, waits):
        grad_rows = grad_outs[layer, y]
        sums[layer, 5:6, :] = column_sum(grad_rows.astype(F32))
        gain_one, gain_two = params[layer, 0:1, :], params[layer, 3:4, :]
        _, unit_one, factor_one = norm_parts(hidden[layer], gain_one, gain_one)
        _, unit_two, factor_two = norm_parts(middles[layer], gain_two, gain_two)
        slot(f"b{layer}_ag")
        wait_all(waits)
        grad_full = grad_outs[layer].reshape(FULL, D)
        grad_up = (dot_nn(grad_full, matrix(wide, layer, 1)) * slopes[layer]).astype(BF16)
        partial = dot_nt(grad_up, matrix(wide, layer, 0))
        waits = scatter_y(links, scatter_out.at[layer, 2], scatter_in.at[layer, 2], partial)
        down_grad = dot_tn(grad_full, actives[layer])
        wide_grads[layer, 1] = down_grad.astype(BF16).reshape(4, 4, SHARD, WIDE)
        up_grad = dot_tn(normed_two[layer].reshape(FULL, D), grad_up)
        wide_grads[layer, 0] = up_grad.astype(BF16).reshape(4, 4, SHARD, WIDE)
        sums[layer, 6:7, :] = column_sum(grad_up.astype(F32))
        slot(f"b{layer}_rs1")
        wait_all(waits)
        grad_two = sum_slots(scatter_in.at[layer, 2])
        grad_middle = grad_rows.astype(F32) + norm_back(grad_two, unit_two, factor_two, gain_two)
        grad_branches[layer, y] = grad_middle.astype(BF16)
        waits = gather_y(links, grad_branches.at[layer])
        sums[layer, 2:3, :] = column_sum(grad_middle)
        sums[layer, 3:4, :] = column_sum(grad_two * unit_two)
        sums[layer, 4:5, :] = column_sum(grad_two)
        slot(f"b{layer}_ag2")
        wait_all(waits)
        branch_full = grad_branches[layer].reshape(FULL, D)
        grad_mixed = dot_nn(branch_full, part(layer, out_part)).astype(BF16).astype(F32)
        stacked_grad = spread_heads(grad_mixed, HD)
        delta = jnp.sum(spread_heads(grad_mixed * attended[layer], HD), axis=1, keepdims=True)
        inverse = 1.0 / totals[layer]
        scaled_grad = (stacked_grad * inverse).astype(BF16)
        stacked_grad = stacked_grad.astype(BF16)
        stacked = queries[layer]

        def chunk_back(chunk, summed):
            keys = pairs[layer, chunk, :, :, 0:256].reshape(CHUNK, 256)
            values = pairs[layer, chunk, :, :, 128:384].reshape(CHUNK, 256)
            weight = probs[layer, chunk]
            products = dot_nt(stacked_grad, values)
            score_grad = (weight.astype(F32) * (products - delta) * inverse).astype(BF16)
            key_grad = dot_tn(score_grad, stacked)
            value_grad = dot_tn(weight, scaled_grad)
            joined = jnp.concatenate(
                [
                    key_grad[:, :128],
                    key_grad[:, 128:] + value_grad[:, :128],
                    value_grad[:, 128:],
                ],
                axis=1,
            )
            pair_grads[layer, chunk] = joined.astype(BF16).reshape(4, FULL, 384)
            return summed + dot_nn(score_grad, keys)

        def chunk_clear(chunk, carry):
            pair_grads[layer, chunk] = jnp.zeros((4, FULL, 384), BF16)
            return carry

        lax.fori_loop(x + 1, 4, chunk_clear, 0)
        query_sum = lax.fori_loop(0, x + 1, chunk_back, jnp.zeros((STACK, 256), F32))
        own = pair_grads.at[layer]
        low, high = pl.ds(0, 64), pl.ds(64, 64)
        waits_a = [
            links.exchange(
                "x",
                steps,
                own.at[links.near("x", steps), :, low],
                pair_in_a.at[layer, x],
                pair_in_a.at[layer, links.near("x", -steps)],
            )
            for steps in (2, 1, 3)
        ]
        waits_b = [
            links.exchange(
                "z",
                steps,
                own.at[:, links.near("z", steps), high],
                pair_in_b.at[layer, z],
                pair_in_b.at[layer, links.near("z", -steps)],
            )
            for steps in (2, 1, 3)
        ]
        pair_in_a[layer, x] = pair_grads[layer, x, :, 0:64]
        pair_in_b[layer, z] = pair_grads[layer, :, z, 64:128]
        grad_query = (join_heads(query_sum, 0) * 0.125).astype(BF16)
        normed = normed_one[layer].reshape(FULL, D)
        query_grad = dot_tn(normed, grad_query)
        out_grad = dot_tn(branch_full, attended[layer].astype(BF16))
        joined = jnp.concatenate(
            [
                query_grad[:, :128],
                query_grad[:, 128:] + out_grad[:, :128],
                out_grad[:, 128:],
            ],
            axis=1,
        )
        narrow_grads[layer, 1] = joined.astype(BF16).reshape(4, 4, SHARD, NARROW)
        partial = dot_nt(grad_query, part(layer, query_part))
        slot(f"b{layer}_kv1")
        wait_all(waits_a)
        pair_mid_a[layer] = sum_slots(pair_in_a.at[layer]).astype(BF16)
        waits_a = [
            links.exchange(
                "z",
                steps,
                pair_mid_a.at[layer, links.near("z", steps)],
                pair_end_a.at[layer, z],
                pair_end_a.at[layer, links.near("z", -steps)],
            )
            for steps in (2, 1, 3)
        ]
        pair_end_a[layer, z] = pair_mid_a[layer, z]
        wait_all(waits_b)
        pair_mid_b[layer] = sum_slots(pair_in_b.at[layer]).astype(BF16)
        waits_b = [
            links.exchange(
                "x",
                steps,
                pair_mid_b.at[layer, links.near("x", steps)],
                pair_end_b.at[layer, x],
                pair_end_b.at[layer, links.near("x", -steps)],
            )
            for steps in (2, 1, 3)
        ]
        pair_end_b[layer, x] = pair_mid_b[layer, x]
        slot(f"b{layer}_kv2")
        wait_all(waits_a)
        wait_all(waits_b)
        grad_pair = jnp.concatenate(
            [sum_slots(pair_end_a.at[layer]), sum_slots(pair_end_b.at[layer])], axis=0
        ).astype(BF16)
        partial = partial + dot_nt(grad_pair, matrix(narrow, layer, 0))
        waits = scatter_y(links, scatter_out.at[layer, 3], scatter_in.at[layer, 3], partial)
        pair_weight_grad = dot_tn(normed, grad_pair)
        narrow_grads[layer, 0] = pair_weight_grad.astype(BF16).reshape(4, 4, SHARD, NARROW)
        sums[layer, 7:8, :] = jnp.concatenate(
            [
                column_sum(grad_pair.astype(F32)),
                column_sum(grad_query.astype(F32)),
                jnp.zeros((1, 128), F32),
            ],
            axis=1,
        )
        slot(f"b{layer}_rs2")
        wait_all(waits)
        grad_one = sum_slots(scatter_in.at[layer, 3])
        sums[layer, 0:1, :] = column_sum(grad_one * unit_one)
        sums[layer, 1:2, :] = column_sum(grad_one)
        grad_input = grad_middle + norm_back(grad_one, unit_one, factor_one, gain_one)
        in_grads[layer] = grad_input.astype(BF16)

    backward(1, cotangent_waits)
    backward(0, gather_grads(0, in_grads[1]))
    in_grad_wait = links.exchange("s", 1, in_grads.at[other], in_grad_cross, in_grad_cross)

    sums_wait = links.exchange("s", 1, sums.at[other], sums_cross, sums_cross)
    tasks["N0"].first()
    sums_wait()
    sums_y[y] = sums[s] + sums_cross[...]
    waits = gather_y(links, sums_y)
    output_wait()
    activations[s] = outputs[s]
    activations[other] = output_cross[...]
    wait_all(waits)
    sums_z[z] = jnp.concatenate([sum_slots(sums_y)[0:6], sums_y[y, 6:8, :]], axis=0)
    waits = [
        links.exchange(
            "z", steps, sums_z.at[z], sums_z.at[z], sums_z.at[links.near("z", -steps)]
        )
        for steps in (1, 3, 2)
    ]
    tasks["N0"].second()
    in_grad_wait()
    input_grads[s] = in_grads[s]
    input_grads[other] = in_grad_cross[...]
    wait_all(waits)
    sums_x[x] = sum_slots(sums_z)
    waits = [
        links.exchange(
            "x", steps, sums_x.at[x], sums_x.at[x], sums_x.at[links.near("x", -steps)]
        )
        for steps in (1, 3, 2)
    ]
    tasks["N0"].last()
    wait_all(waits)
    param_grads[...] = sum_slots(sums_x)
    for layer in range(2):
        tasks[f"W{layer}"].finish()
        tasks[f"N{layer}"].finish()
    wide_out[s] = wide_done[s]
    wide_out[other] = wide_other[s]
    narrow_out[s] = narrow_done[s]
    narrow_out[other] = narrow_other[s]
    links.finish()


def scratch_shapes():
    def low(*shape):
        return pltpu.VMEM(shape, BF16)

    def full(*shape):
        return pltpu.VMEM(shape, F32)

    return [
        pltpu.SemaphoreType.DMA((SEMS,)),
        pltpu.SemaphoreType.DMA((SEMS,)),
        low(2, SHARD, WIDE),
        low(2, SHARD, NARROW),
        low(2, 2, 4, 4, SHARD, WIDE),
        low(2, 2, 4, 4, SHARD, NARROW),
        full(2, 8, D),
        low(2, 4, ROWS, D),
        low(2, 4, ROWS, D),
        low(2, 4, ROWS, D),
        low(2, 4, ROWS, D),
        low(2, 4, 4, ROWS, D),
        low(2, 4, 4, ROWS, D),
        low(2, 4, 4, FULL, 384),
        full(4, STACK, CHUNK),
        low(2, 4, STACK, CHUNK),
        low(2, STACK, 256),
        full(2, STACK, 1),
        full(2, FULL, 256),
        full(2, ROWS, D),
        full(2, ROWS, D),
        low(2, FULL, D),
        full(2, FULL, D),
        low(2, 4, 4, FULL, 384),
        low(2, 4, 4, 64, 384),
        low(2, 4, 4, 64, 384),
        low(2, 4, 64, 384),
        low(2, 4, 64, 384),
        low(2, 4, 64, 384),
        low(2, 4, 64, 384),
        low(2, 2, 4, 4, SHARD, WIDE),
        low(2, 2, 4, 4, SHARD, NARROW),
        low(2, 4, 4, SHARD, WIDE),
        low(2, 4, 4, SHARD, WIDE),
        low(2, 4, 4, SHARD, WIDE),
        low(2, 4, SHARD, WIDE),
        low(2, 4, SHARD, WIDE),
        full(2, SHARD, WIDE),
        full(2, SHARD, WIDE),
        low(2, 4, 4, SHARD, NARROW),
        low(2, 4, 4, SHARD, NARROW),
        low(2, 4, 4, SHARD, NARROW),
        low(2, 4, SHARD, NARROW),
        low(2, 4, SHARD, NARROW),
        full(2, SHARD, NARROW),
        full(2, SHARD, NARROW),
        full(2, 8, D),
        full(8, D),
        full(4, 8, D),
        full(4, 8, D),
        full(4, 8, D),
        low(2, ROWS, D),
        low(ROWS, D),
        low(2, ROWS, D),
        low(ROWS, D),
    ]


def result_kernel(
    acts,
    in_grads,
    wide,
    narrow,
    sums,
    activations,
    input_grads,
    ln1_gain,
    ln1_bias,
    w_qkv,
    b_qv,
    w_out,
    b_out,
    ln2_gain,
    ln2_bias,
    w_up,
    b_up,
    w_down,
    b_down,
):
    activations[0] = acts[...]
    input_grads[0] = in_grads[...]
    rows = (ln1_gain, ln1_bias, b_out, ln2_gain, ln2_bias, b_down, b_up)
    for index, target in enumerate(rows):
        target[...] = sums[index : index + 1, :]
    b_qv[0, 0:1, :] = sums[7:8, 384:576]
    b_qv[0, 1:2, :] = sums[7:8, 192:384]
    w_up[0] = wide[0]
    w_down[0] = wide[1]
    w_qkv[0, 0] = narrow[1, :, :192]
    w_qkv[0, 1] = narrow[0, :, :192]
    w_qkv[0, 2] = narrow[0, :, 192:]
    w_out[0] = narrow[1, :, 192:]


def model_rows_first(arrays):
    arrays = list(arrays)
    for index in (4, 6, 12):
        arrays[index] = jnp.swapaxes(arrays[index], 1, 2)
    return arrays


def local(*arrays):
    arrays = model_rows_first(arrays)
    whole = pl.BlockSpec(memory_space=pltpu.VMEM)
    results = pl.pallas_call(
        kernel,
        name="layers",
        out_shape=(
            jax.ShapeDtypeStruct((2, ROWS, D), BF16),
            jax.ShapeDtypeStruct((2, ROWS, D), BF16),
            jax.ShapeDtypeStruct((2, SHARD, WIDE), F32),
            jax.ShapeDtypeStruct((2, SHARD, NARROW), F32),
            jax.ShapeDtypeStruct((8, D), F32),
        ),
        in_specs=[whole] * 14,
        out_specs=(whole,) * 5,
        scratch_shapes=scratch_shapes(),
        compiler_params=pltpu.CompilerParams(
            collective_id=0, has_side_effects=True, vmem_limit_bytes=60 * 2**20
        ),
    )(*arrays)
    rows = jax.ShapeDtypeStruct((1, 2, ROWS, D), BF16)
    shapes = [rows, rows] + [jax.ShapeDtypeStruct(a.shape, F32) for a in arrays[2:]]
    results = pl.pallas_call(
        result_kernel,
        name="results",
        out_shape=shapes,
        in_specs=[whole] * 5,
        out_specs=[whole] * 14,
    )(*results)
    return tuple(model_rows_first(results))


def solution(mesh):
    rows = P(None, ("gx", "gy"), None)
    vector = P("section", None)
    qkv = P("section", "gx", None, "gy")
    bias_qv = P("section", None, "gy")
    out = P("section", "gy", "gx")
    up = P("section", "gx", "gy")
    hidden = P("section", "gy")
    sharded = (vector, vector, qkv, bias_qv, out, vector, vector, vector, up, hidden, out, vector)
    layer_rows = P("section", None, ("gx", "gy"), None)
    return jax.shard_map(
        local,
        mesh=mesh,
        in_specs=(rows, rows) + sharded,
        out_specs=(layer_rows, layer_rows) + sharded,
        check_vma=False,
    )
```

```python
import jax
import jax.numpy as jnp
from jax import lax
from jax.experimental import pallas as pl
from jax.experimental.pallas import tpu as pltpu
from jax.sharding import PartitionSpec as P

HD = 64
EPSILON = 1e-05
MASKED = -1e30
MESH = pl.DeviceIdType.MESH
F32 = jnp.float32
BF16 = jnp.bfloat16

ROWS = 32
FULL = 128
D = 768
CHUNK = 512
HEADS = 3
STACK = HEADS * FULL

WIDE = 768
NARROW = 256
SHARD = 48
SEMS = 320


def dot_nn(a, b):
    return lax.dot_general(a, b, (((1,), (0,)), ((), ())), preferred_element_type=F32)


def dot_nt(a, b):
    return lax.dot_general(a, b, (((1,), (1,)), ((), ())), preferred_element_type=F32)


def dot_tn(a, b):
    return lax.dot_general(a, b, (((0,), (0,)), ((), ())), preferred_element_type=F32)


def norm_parts(values, gain, offset):
    average = jnp.mean(values, axis=-1, keepdims=True)
    centered = values - average
    variance = jnp.mean(centered * centered, axis=-1, keepdims=True)
    factor = lax.rsqrt(variance + EPSILON)
    unit_rows = centered * factor
    return (unit_rows * gain + offset, unit_rows, factor)


def norm_back(grad_rows, unit_rows, factor, gain):
    scaled = grad_rows * gain
    first_mean = jnp.mean(scaled, axis=-1, keepdims=True)
    second_mean = jnp.mean(scaled * unit_rows, axis=-1, keepdims=True)
    return factor * (scaled - first_mean - unit_rows * second_mean)


def gelu_parts(values):
    scale = 0.7978845608028654
    inner = scale * (values + 0.044715 * values * values * values)
    bent = jnp.tanh(inner)
    active = 0.5 * values * (1.0 + bent)
    slope = 0.5 * (1.0 + bent) + 0.5 * values * (1.0 - bent * bent) * scale * (
        1.0 + 3.0 * 0.044715 * values * values
    )
    return active, slope


def column_sum(values):
    return jnp.sum(values, axis=0, keepdims=True)


def head_mask(head, first):
    lane = lax.broadcasted_iota(jnp.int32, (FULL, 256), 1)
    low = first + HD * head
    return jnp.logical_and(lane >= low, lane < low + HD)


def spread_heads(values, first):
    return jnp.concatenate(
        [jnp.where(head_mask(head, first), values, 0.0) for head in range(HEADS)], axis=0
    )


def join_heads(stacked, first):
    total = jnp.zeros((FULL, 256), F32)
    for head in range(HEADS):
        part = stacked[head * FULL : (head + 1) * FULL]
        total = total + jnp.where(head_mask(head, first), part, 0.0)
    return total


def only_if(condition, action):
    if condition is None:
        action()
    else:
        pl.when(condition)(lambda: action())


class Links:
    def __init__(self, send_sems, recv_sems):
        self.send_sems, self.recv_sems = send_sems, recv_sems
        self.count = 0
        self.sent = []
        self.section = lax.axis_index("section")
        self.row = lax.axis_index("gx")
        self.y = lax.axis_index("gy")
        self.x = self.row // 4
        self.z = self.row % 4

    def near(self, axis, steps):
        if axis == "s":
            return 1 - self.section
        return (getattr(self, axis) + (steps + 4)) % 4

    def place(self, first, second):
        s = self.section
        x = (self.x + (first + 4) * s + (second + 4) * (1 - s)) % 4
        z = (self.z + (first + 4) * (1 - s) + (second + 4) * s) % 4
        return x, z

    def device(self, axis, steps):
        s, x, z, y = self.section, self.x, self.z, self.y
        if axis == "first":
            x, z = self.place(steps, 0)
            return (s, x * 4 + z, y)
        if axis == "second":
            x, z = self.place(0, steps)
            return (s, x * 4 + z, y)
        there = self.near(axis, steps)
        if axis == "s":
            s = there
        elif axis == "x":
            x = there
        elif axis == "z":
            z = there
        else:
            y = there
        return (s, x * 4 + z, y)

    def exchange(self, axis, steps, source, target, landing, send_if=None, come_if=None):
        index = self.count
        self.count += 1
        sems = (self.send_sems.at[index], self.recv_sems.at[index])
        copy = pltpu.make_async_remote_copy(
            source, target, *sems, device_id=self.device(axis, steps), device_id_type=MESH
        )
        only_if(send_if, copy.start)
        self.sent.append((send_if, copy.wait_send))
        arrival = pltpu.make_async_remote_copy(
            landing, landing, *sems, device_id=self.device(axis, -steps), device_id_type=MESH
        )
        return lambda: only_if(come_if, arrival.wait_recv)

    def barrier(self):
        barrier = pltpu.get_barrier_semaphore()
        peers = [("s", 1)] + [(axis, steps) for axis in "xyz" for steps in (1, 2, 3)]
        for axis, steps in peers:
            pl.semaphore_signal(
                barrier, inc=1, device_id=self.device(axis, steps), device_id_type=MESH
            )
        pl.semaphore_wait(barrier, len(peers))

    def finish(self):
        for condition, wait in self.sent:
            only_if(condition, wait)
        self.sent = []


def wait_all(waits):
    for wait in waits:
        wait()


def gather_y(links, buffer):
    y = links.y
    return [
        links.exchange("y", steps, buffer.at[y], buffer.at[y], buffer.at[links.near("y", -steps)])
        for steps in (1, 3, 2)
    ]


def scatter_y(links, outgoing, incoming, partial):
    y = links.y
    outgoing[...] = partial.astype(BF16).reshape(4, ROWS, D)
    waits = [
        links.exchange(
            "y",
            steps,
            outgoing.at[links.near("y", steps)],
            incoming.at[y],
            incoming.at[links.near("y", -steps)],
        )
        for steps in (2, 1, 3)
    ]
    incoming[y] = outgoing[y]
    return waits


def sum_slots(buffer):
    total = buffer[0].astype(F32)
    for slot in range(1, 4):
        total = total + buffer[slot].astype(F32)
    return total


SCHEDULE = {
    "x": ("q0.begin", "q0.own"),
    "f0_q": ("q0.forward", "w0.begin", "w0.own"),
    "f0_kv": ("q0.cross", "w0.forward"),
    "f0_rs1": ("w0.cross", "k1.begin", "k1.own"),
    "f0_ag2": ("k1.forward", "q1.begin", "q1.own", "w1.begin", "w1.own"),
    "f0_rs2": ("k1.cross", "q1.forward", "w1.forward"),
    "f1_q": ("q1.cross",),
    "f1_rs1": ("w1.cross",),
    "b1_kv1": ("W1.begin", "Q1.begin"),
    "b1_rs2": ("K1.begin", "W1.first"),
    "b0_ag": ("Q1.first", "K1.first"),
    "b0_rs1": ("W0.begin", "W1.second"),
    "b0_ag2": ("W0.first", "Q1.second", "K1.second"),
    "b0_kv1": ("Q0.begin",),
    "b0_kv2": ("W0.second", "Q0.first", "W1.last", "Q1.last", "K1.last"),
    "b0_rs2": ("K0.begin", "W0.last", "Q0.second"),
}
RELAYED = ()


class Gather:
    def __init__(self, links, buffer, layer, relayed):
        self.links, self.buffer, self.layer = links, buffer, layer
        self.relayed = relayed
        self.near = []
        self.far = []

    def block(self, first, second):
        x, z = self.links.place(first, second)
        return self.buffer.at[self.layer, self.links.section, x, z]

    def begin(self):
        own = self.block(0, 0)
        self.first = [
            self.links.exchange("first", steps, own, own, self.block(-steps, 0))
            for steps in (1, 3, 2)
        ]

    def send(self, first):
        came = self.block(-first, 0)
        for steps in (1, 3) if self.relayed else (1, 3, 2):
            wait = self.links.exchange("second", steps, came, came, self.block(-first, -steps))
            (self.near if steps != 2 else self.far).append(wait)

    def own(self):
        self.send(0)

    def forward(self):
        for wait, first in zip(self.first, (1, 3, 2)):
            wait()
            self.send(first)

    def relay(self):
        wait_all(self.near)
        self.near = []
        if self.relayed:
            for first, steps in zip((0, 1, 3, 2), (1, 3, 1, 3)):
                came = self.block(-first, -steps)
                self.far.append(
                    self.links.exchange("second", steps, came, came, self.block(-first, -2))
                )

    def cross(self):
        wait_all(self.near + self.far)
        s = self.links.section
        mine = self.buffer.at[self.layer, s]
        self.finish = self.links.exchange("s", 1, mine, mine, self.buffer.at[self.layer, 1 - s])


class Scatter:
    def __init__(self, links, layer, grads, crossed, work, arrived, middle, ended, done, other):
        self.links, self.layer, self.grads, self.crossed = links, layer, grads, crossed
        self.work, self.arrived, self.middle, self.ended = work, arrived, middle, ended
        self.done, self.other = done.at[layer], other.at[layer]
        s, x, z = links.section, links.x, links.z
        self.first_index = z * (1 - s) + x * s
        self.second_index = x * (1 - s) + z * s

    def begin(self):
        s = self.links.section
        self.crossing = self.links.exchange(
            "s", 1, self.grads.at[self.layer, 1 - s], self.crossed, self.crossed
        )

    def spread(self, axis, index, source, target):
        waits = []
        for steps in (2, 1, 3):
            waits.append(
                self.links.exchange(
                    axis,
                    steps,
                    source.at[(index + steps) % 4],
                    target.at[index],
                    target.at[(index + 4 - steps) % 4],
                )
            )
        target[index] = source[index]
        return waits

    def first(self):
        self.crossing()
        s = self.links.section

        def add(first, carry):
            for second in range(4):
                x = first * s + second * (1 - s)
                z = first * (1 - s) + second * s
                mine = self.grads[self.layer, s, x, z].astype(F32)
                self.work[first, second] = (mine + self.crossed[x, z].astype(F32)).astype(BF16)
            return carry

        lax.fori_loop(0, 4, add, 0)
        self.waits = self.spread("first", self.first_index, self.work, self.arrived)

    def second(self):
        wait_all(self.waits)
        self.middle[...] = sum_slots(self.arrived).astype(BF16)
        self.waits = self.spread("second", self.second_index, self.middle, self.ended)

    def last(self):
        wait_all(self.waits)
        self.done[...] = sum_slots(self.ended)
        self.finish = self.links.exchange("s", 1, self.done, self.other, self.other)


def kernel(
    inputs,
    cotangent,
    ln1_gain,
    ln1_bias,
    w_qkv,
    b_qv,
    w_out,
    b_out,
    ln2_gain,
    ln2_bias,
    w_up,
    b_up,
    w_down,
    b_down,
    activations,
    input_grads,
    wide_out,
    joint_out,
    side_out,
    param_grads,
    send_sems,
    recv_sems,
    own_wide,
    own_joint,
    own_side,
    wide,
    joint,
    side,
    params,
    normed_one,
    normed_two,
    units,
    grad_outs,
    grad_branches,
    scatter_out,
    scatter_in,
    pairs,
    scores,
    probs,
    queries,
    query_sums,
    tops,
    totals,
    attended,
    hidden,
    middles,
    actives,
    slopes,
    pair_grads,
    pair_in_a,
    pair_in_b,
    pair_mid_a,
    pair_mid_b,
    pair_end_a,
    pair_end_b,
    wide_grads,
    joint_grads,
    side_grads,
    wide_crossed,
    wide_work,
    wide_arrived,
    wide_middle,
    wide_ended,
    wide_done,
    wide_other,
    joint_crossed,
    joint_work,
    joint_arrived,
    joint_middle,
    joint_ended,
    joint_done,
    joint_other,
    side_crossed,
    side_work,
    side_arrived,
    side_middle,
    side_ended,
    side_done,
    side_other,
    sums,
    sums_cross,
    sums_y,
    sums_z,
    sums_x,
    outputs,
    output_cross,
    in_grads,
    in_grad_cross,
):
    links = Links(send_sems, recv_sems)
    s, x, z, y, row = links.section, links.x, links.z, links.y, links.row
    other = 1 - s
    own_wide[0] = w_up[0]
    own_wide[1] = w_down[0]
    none = jnp.zeros((SHARD, 64), BF16)
    own_joint[0] = jnp.concatenate([w_qkv[0, 1], none], axis=1)
    own_joint[1] = jnp.concatenate([none, w_qkv[0, 2]], axis=1)
    own_side[0] = jnp.concatenate([w_qkv[0, 0], none], axis=1)
    own_side[1] = jnp.concatenate([none, w_out[0]], axis=1)
    rows = (ln1_gain, ln1_bias, b_out, ln2_gain, ln2_bias, b_down, b_up)
    for index, values in enumerate(rows):
        params[s, index : index + 1, :] = values[...]
    blank = jnp.zeros((1, 192), F32)
    params[s, 7:8, :] = jnp.concatenate([blank, b_qv[0, 1:2], b_qv[0, 0:1], blank], axis=1)
    wide[s, :, x, z] = own_wide[...]
    joint[s, :, x, z] = own_joint[...]
    side[s, :, x, z] = own_side[...]
    links.barrier()

    joint_wait = links.exchange(
        "s", 1, own_joint.at[other], joint.at[s, other, x, z], joint.at[other, s, x, z]
    )
    params_wait = links.exchange("s", 1, params.at[s], params.at[s], params.at[other])
    side_wait = links.exchange(
        "s", 1, own_side.at[other], side.at[s, other, x, z], side.at[other, s, x, z]
    )
    wide_wait = links.exchange(
        "s", 1, own_wide.at[other], wide.at[s, other, x, z], wide.at[other, s, x, z]
    )
    tasks = {}
    for layer in range(2):
        for name, buffer in (("k", joint), ("q", side), ("w", wide)):
            name = name + str(layer)
            tasks[name] = Gather(links, buffer, layer, name in RELAYED)

    def slot(name):
        for step in SCHEDULE.get(name, ()):
            task, action = step.split(".")
            getattr(tasks[task], action)()

    joint_wait()
    tasks["k0"].begin()
    tasks["k0"].own()
    params_wait()

    def gather_hidden(layer, current):
        hidden[layer, y] = current
        waits = gather_y(links, hidden.at[layer])
        slot(f"f{layer}_ag")
        return waits

    hidden_waits = gather_hidden(0, inputs[s])

    side_wait()
    wide_wait()
    tasks["k0"].forward()
    slot("w")
    tasks["k0"].relay()
    tasks["k0"].cross()
    slot("x")

    def matrix(buffer, layer, half):
        return buffer[layer, half].reshape(D, buffer.shape[-1])

    def gather_grads(layer, grad_rows):
        grad_outs[layer, y] = grad_rows
        return gather_y(links, grad_outs.at[layer])

    def forward(layer, hidden_waits):
        wait_all(hidden_waits)
        hidden_full = hidden[layer].reshape(FULL, D).astype(F32)
        normed, unit_rows, _ = norm_parts(hidden_full, params[layer, 0:1, :], params[layer, 1:2, :])
        normed = normed.astype(BF16)
        normed_one[layer] = normed
        units[layer] = unit_rows.reshape(4, ROWS, D)
        tasks[f"k{layer}"].finish()
        key = dot_nn(normed, matrix(joint, layer, 0))
        value = dot_nn(normed, matrix(joint, layer, 1))
        pair = jnp.concatenate(
            [key[:, :128], key[:, 128:] + value[:, :128], value[:, 128:]], axis=1
        )
        pair = pair + params[layer, 7:8, 0:384]
        pairs[layer, x, z] = pair.astype(BF16)
        own = pairs.at[layer]
        low, high = pl.ds(0, 64), pl.ds(64, 64)
        pair_waits = {steps: [] for steps in range(4)}

        def pairs_x(column, half):
            for steps in (1, 3, 2):
                yield steps, links.exchange(
                    "x",
                    steps,
                    own.at[x, column, half],
                    own.at[x, column, half],
                    own.at[links.near("x", -steps), column, half],
                    x <= 3 - steps,
                    x >= steps,
                )

        def pairs_z(plane, half, condition):
            for steps in (1, 3, 2):
                yield steps, links.exchange(
                    "z",
                    steps,
                    own.at[plane, z, half],
                    own.at[plane, z, half],
                    own.at[plane, links.near("z", -steps), half],
                    condition,
                    condition,
                )

        pair_first_a = list(pairs_z(x, low, None))
        pair_first_b = list(pairs_x(z, high))
        for steps, wait in pairs_x(z, low):
            pair_waits[steps].append(wait)
        pair_waits[0] += [wait for _, wait in pairs_z(x, high, None)]
        slot(f"f{layer}_q")
        for (steps_a, wait_a), (steps_b, wait_b) in zip(pair_first_a, pair_first_b):
            wait_a()
            for steps, wait in pairs_x(links.near("z", -steps_a), low):
                pair_waits[steps].append(wait)
            wait_b()
            came = links.near("x", -steps_b)
            pair_waits[steps_b] += [wait for _, wait in pairs_z(came, high, x >= steps_b)]
        slot(f"f{layer}_kv")
        tasks[f"q{layer}"].finish()
        query = dot_nn(normed, matrix(side, layer, 0)) + params[layer, 7:8, 384:640]
        query = query.astype(BF16).astype(F32) * 0.125
        queries[layer] = spread_heads(query, 0).astype(BF16)

        stacked = queries[layer]
        position = lax.broadcasted_iota(jnp.int32, (STACK, CHUNK), 0) % FULL + row * FULL
        column = lax.broadcasted_iota(jnp.int32, (STACK, CHUNK), 1)

        def find_top(chunk):
            keys = pairs[layer, chunk, :, :, 0:256].reshape(CHUNK, 256)
            raw = dot_nt(stacked, keys)
            raw = jnp.where(column + chunk * CHUNK <= position, raw, MASKED)
            scores[chunk] = raw
            tops[...] = jnp.maximum(tops[...], jnp.max(raw, axis=1, keepdims=True))

        tops[...] = jnp.full((STACK, 1), MASKED, F32)
        for steps in (0, 1, 3, 2):
            wait_all(pair_waits[steps])
            chunk = links.near("x", -steps)
            only_if(None if steps == 0 else x >= steps, lambda: find_top(chunk))
        top = tops[...]

        def add_chunk(chunk, carry):
            total, summed = carry
            weight = jnp.exp(scores[chunk] - top)
            rounded = weight.astype(BF16)
            probs[layer, chunk] = rounded
            values = pairs[layer, chunk, :, :, 128:384].reshape(CHUNK, 256)
            return (
                total + jnp.sum(weight, axis=1, keepdims=True),
                summed + dot_nn(rounded, values),
            )

        total, summed = lax.fori_loop(
            0, x + 1, add_chunk, (jnp.zeros((STACK, 1), F32), jnp.zeros((STACK, 256), F32))
        )
        totals[layer] = total
        attention = join_heads(summed / total, HD)
        attended[layer] = attention
        partial = dot_nt(attention.astype(BF16), matrix(side, layer, 1))
        waits = scatter_y(links, scatter_out.at[layer, 0], scatter_in.at[layer, 0], partial)
        slot(f"f{layer}_rs1")
        wait_all(waits)
        middle = hidden[layer, y].astype(F32) + sum_slots(scatter_in.at[layer, 0])
        middle = middle + params[layer, 2:3, :]
        middles[layer, y] = middle
        second, _, _ = norm_parts(middle, params[layer, 3:4, :], params[layer, 4:5, :])
        normed_two[layer, y] = second.astype(BF16)
        waits = gather_y(links, normed_two.at[layer])
        slot(f"f{layer}_ag2")
        wait_all(waits)
        tasks[f"w{layer}"].finish()
        upward = (
            dot_nn(normed_two[layer].reshape(FULL, D), matrix(wide, layer, 0)) + params[layer, 6:7, :]
        )
        active, slope = gelu_parts(upward)
        actives[layer] = active.astype(BF16)
        slopes[layer] = slope
        partial = dot_nt(actives[layer], matrix(wide, layer, 1))
        waits = scatter_y(links, scatter_out.at[layer, 1], scatter_in.at[layer, 1], partial)
        slot(f"f{layer}_rs2")
        wait_all(waits)
        result = middles[layer, y] + sum_slots(scatter_in.at[layer, 1]) + params[layer, 5:6, :]
        outputs[layer] = result.astype(BF16)

    forward(0, hidden_waits)
    cotangent_waits = gather_grads(1, cotangent[s])
    forward(1, gather_hidden(1, outputs[0]))
    output_wait = links.exchange("s", 1, outputs.at[other], output_cross, output_cross)

    def scatters(layer):
        wide_scatter = Scatter(
            links,
            layer,
            wide_grads,
            wide_crossed.at[layer],
            wide_work.at[layer],
            wide_arrived.at[layer],
            wide_middle.at[layer],
            wide_ended.at[layer],
            wide_done,
            wide_other,
        )
        joint_scatter = Scatter(
            links,
            layer,
            joint_grads,
            joint_crossed.at[layer],
            joint_work.at[layer],
            joint_arrived.at[layer],
            joint_middle.at[layer],
            joint_ended.at[layer],
            joint_done,
            joint_other,
        )
        side_scatter = Scatter(
            links,
            layer,
            side_grads,
            side_crossed.at[layer],
            side_work.at[layer],
            side_arrived.at[layer],
            side_middle.at[layer],
            side_ended.at[layer],
            side_done,
            side_other,
        )
        return wide_scatter, joint_scatter, side_scatter

    for layer in range(2):
        tasks[f"W{layer}"], tasks[f"K{layer}"], tasks[f"Q{layer}"] = scatters(layer)

    sum_waits = []

    def backward(layer, waits):
        grad_rows = grad_outs[layer, y]
        sums[layer, 5:6, :] = column_sum(grad_rows.astype(F32))
        gain_one, gain_two = params[layer, 0:1, :], params[layer, 3:4, :]
        _, unit_one, factor_one = norm_parts(hidden[layer, y].astype(F32), gain_one, gain_one)
        _, unit_two, factor_two = norm_parts(middles[layer, y], gain_two, gain_two)
        slot(f"b{layer}_ag")
        wait_all(waits)
        grad_full = grad_outs[layer].reshape(FULL, D)
        grad_up = (dot_nn(grad_full, matrix(wide, layer, 1)) * slopes[layer]).astype(BF16)
        partial = dot_nt(grad_up, matrix(wide, layer, 0))
        waits = scatter_y(links, scatter_out.at[layer, 2], scatter_in.at[layer, 2], partial)
        down_grad = dot_tn(grad_full, actives[layer])
        wide_grads[layer, 1] = down_grad.astype(BF16).reshape(4, 4, SHARD, WIDE)
        up_grad = dot_tn(normed_two[layer].reshape(FULL, D), grad_up)
        wide_grads[layer, 0] = up_grad.astype(BF16).reshape(4, 4, SHARD, WIDE)
        sums[layer, 6:7, :] = column_sum(grad_up.astype(F32))
        slot(f"b{layer}_rs1")
        wait_all(waits)
        grad_two = sum_slots(scatter_in.at[layer, 2])
        grad_middle = grad_rows.astype(F32) + norm_back(grad_two, unit_two, factor_two, gain_two)
        grad_branches[layer, y] = grad_middle.astype(BF16)
        waits = gather_y(links, grad_branches.at[layer])
        sums[layer, 2:3, :] = column_sum(grad_middle)
        sums[layer, 3:4, :] = column_sum(grad_two * unit_two)
        sums[layer, 4:5, :] = column_sum(grad_two)
        slot(f"b{layer}_ag2")
        wait_all(waits)
        branch_full = grad_branches[layer].reshape(FULL, D)
        grad_mixed = dot_nn(branch_full, matrix(side, layer, 1)).astype(BF16).astype(F32)
        stacked_grad = spread_heads(grad_mixed, HD)
        delta = jnp.sum(spread_heads(grad_mixed * attended[layer], HD), axis=1, keepdims=True)
        inverse = 1.0 / totals[layer]
        scaled_grad = (stacked_grad * inverse).astype(BF16)
        stacked_grad = stacked_grad.astype(BF16)
        stacked = queries[layer]

        own = pair_grads.at[layer]
        low, high = pl.ds(0, 64), pl.ds(64, 64)
        waits_a, waits_b = [], []

        def chunk_back(chunk):
            keys = pairs[layer, chunk, :, :, 0:256].reshape(CHUNK, 256)
            values = pairs[layer, chunk, :, :, 128:384].reshape(CHUNK, 256)
            weight = probs[layer, chunk]
            products = dot_nt(stacked_grad, values)
            score_grad = (weight.astype(F32) * (products - delta) * inverse).astype(BF16)
            key_grad = dot_tn(score_grad, stacked)
            value_grad = dot_tn(weight, scaled_grad)
            joined = jnp.concatenate(
                [
                    key_grad[:, :128],
                    key_grad[:, 128:] + value_grad[:, :128],
                    value_grad[:, 128:],
                ],
                axis=1,
            )
            pair_grads[layer, chunk] = joined.astype(BF16).reshape(4, FULL, 384)
            pair_in_b[layer, z, chunk] = pair_grads[layer, chunk, z, 64:128]
            query_sums[...] = query_sums[...] + dot_nn(score_grad, keys)

        def earlier(chunk):
            chunk_back(chunk)
            pair_in_a[layer, chunk] = jnp.zeros((4, 64, 384), BF16)
            pair_end_b[layer, chunk] = jnp.zeros((64, 384), BF16)

        def send_z(chunk, condition):
            for steps in (2, 1, 3):
                waits_b.append(
                    links.exchange(
                        "z",
                        steps,
                        own.at[chunk, links.near("z", steps), high],
                        pair_in_b.at[layer, z, chunk],
                        pair_in_b.at[layer, links.near("z", -steps), chunk],
                        condition,
                        condition,
                    )
                )

        query_sums[...] = jnp.zeros((STACK, 256), F32)
        for steps in (3, 2, 1):
            chunk = links.near("x", -steps)
            pl.when(x >= steps)(lambda: earlier(chunk))
            waits_a.append(
                links.exchange(
                    "x",
                    -steps,
                    own.at[chunk, :, low],
                    pair_in_a.at[layer, x],
                    pair_in_a.at[layer, links.near("x", steps)],
                    x >= steps,
                    x <= 3 - steps,
                )
            )
            send_z(chunk, x >= steps)
        chunk_back(x)
        send_z(x, None)
        pair_in_a[layer, x] = pair_grads[layer, x, :, 0:64]
        query_sum = query_sums[...]
        grad_query = (join_heads(query_sum, 0) * 0.125).astype(BF16)
        normed = normed_one[layer]
        query_grad = dot_tn(normed, grad_query)
        side_grads[layer, 0] = query_grad.astype(BF16).reshape(4, 4, SHARD, NARROW)
        out_grad = dot_tn(branch_full, attended[layer].astype(BF16))
        side_grads[layer, 1] = out_grad.astype(BF16).reshape(4, 4, SHARD, NARROW)
        partial = dot_nt(grad_query, matrix(side, layer, 0))
        slot(f"b{layer}_kv1")
        wait_all(waits_a)
        pair_mid_a[layer] = sum_slots(pair_in_a.at[layer]).astype(BF16)
        waits_a = [
            links.exchange(
                "z",
                steps,
                pair_mid_a.at[layer, links.near("z", steps)],
                pair_end_a.at[layer, z],
                pair_end_a.at[layer, links.near("z", -steps)],
            )
            for steps in (2, 1, 3)
        ]
        pair_end_a[layer, z] = pair_mid_a[layer, z]
        wait_all(waits_b)

        def sum_chunk(chunk):
            pair_mid_b[layer, chunk] = sum_slots(pair_in_b.at[layer, :, chunk]).astype(BF16)

        waits_b = []
        for steps in (3, 2, 1):
            chunk = links.near("x", -steps)
            pl.when(x >= steps)(lambda: sum_chunk(chunk))
            waits_b.append(
                links.exchange(
                    "x",
                    -steps,
                    pair_mid_b.at[layer, chunk],
                    pair_end_b.at[layer, x],
                    pair_end_b.at[layer, links.near("x", steps)],
                    x >= steps,
                    x <= 3 - steps,
                )
            )
        sum_chunk(x)
        pair_end_b[layer, x] = pair_mid_b[layer, x]
        slot(f"b{layer}_kv2")
        wait_all(waits_a)
        wait_all(waits_b)
        grad_pair = jnp.concatenate(
            [sum_slots(pair_end_a.at[layer]), sum_slots(pair_end_b.at[layer])], axis=0
        ).astype(BF16)
        partial = partial + dot_nt(grad_pair[:, 0:256], matrix(joint, layer, 0))
        partial = partial + dot_nt(grad_pair[:, 128:384], matrix(joint, layer, 1))
        waits = scatter_y(links, scatter_out.at[layer, 3], scatter_in.at[layer, 3], partial)
        key_weight_grad = dot_tn(normed, grad_pair[:, 0:256])
        joint_grads[layer, 0] = key_weight_grad.astype(BF16).reshape(4, 4, SHARD, NARROW)
        value_weight_grad = dot_tn(normed, grad_pair[:, 128:384])
        joint_grads[layer, 1] = value_weight_grad.astype(BF16).reshape(4, 4, SHARD, NARROW)
        sums[layer, 0:1, :] = column_sum(partial * units[layer].reshape(FULL, D))
        sums[layer, 1:2, :] = column_sum(partial)
        sums[layer, 7:8, :] = jnp.concatenate(
            [
                column_sum(grad_pair.astype(F32)),
                column_sum(grad_query.astype(F32)),
                jnp.zeros((1, 128), F32),
            ],
            axis=1,
        )
        slot(f"b{layer}_rs2")
        if layer == 0:
            sums_wait = links.exchange("s", 1, sums.at[other], sums_cross, sums_cross)
            sums_wait()
            sums_y[y] = sums[s] + sums_cross[...]
            sum_waits.extend(gather_y(links, sums_y))
        wait_all(waits)
        grad_one = sum_slots(scatter_in.at[layer, 3])
        grad_input = grad_middle + norm_back(grad_one, unit_one, factor_one, gain_one)
        in_grads[layer] = grad_input.astype(BF16)

    backward(1, cotangent_waits)
    backward(0, gather_grads(0, in_grads[1]))
    in_grad_wait = links.exchange("s", 1, in_grads.at[other], in_grad_cross, in_grad_cross)

    tasks["K0"].first()
    output_wait()
    activations[s] = outputs[s]
    activations[other] = output_cross[...]
    wait_all(sum_waits)
    sums_z[z] = jnp.concatenate([sum_slots(sums_y)[0:6], sums_y[y, 6:8, :]], axis=0)
    waits = [
        links.exchange(
            "z", steps, sums_z.at[z], sums_z.at[z], sums_z.at[links.near("z", -steps)]
        )
        for steps in (1, 3, 2)
    ]
    tasks["Q0"].last()
    tasks["K0"].second()
    in_grad_wait()
    input_grads[s] = in_grads[s]
    input_grads[other] = in_grad_cross[...]
    wait_all(waits)
    sums_x[x] = sum_slots(sums_z)
    waits = [
        links.exchange(
            "x", steps, sums_x.at[x], sums_x.at[x], sums_x.at[links.near("x", -steps)]
        )
        for steps in (1, 3, 2)
    ]
    tasks["K0"].last()
    wait_all(waits)
    param_grads[...] = sum_slots(sums_x)
    for layer in range(2):
        tasks[f"W{layer}"].finish()
        tasks[f"K{layer}"].finish()
        tasks[f"Q{layer}"].finish()
    wide_out[s] = wide_done[s]
    wide_out[other] = wide_other[s]
    joint_out[s] = joint_done[s]
    joint_out[other] = joint_other[s]
    side_out[s] = side_done[s]
    side_out[other] = side_other[s]
    links.finish()


def scratch_shapes():
    def low(*shape):
        return pltpu.VMEM(shape, BF16)

    def full(*shape):
        return pltpu.VMEM(shape, F32)

    return [
        pltpu.SemaphoreType.DMA((SEMS,)),
        pltpu.SemaphoreType.DMA((SEMS,)),
        low(2, SHARD, WIDE),
        low(2, SHARD, NARROW),
        low(2, SHARD, NARROW),
        low(2, 2, 4, 4, SHARD, WIDE),
        low(2, 2, 4, 4, SHARD, NARROW),
        low(2, 2, 4, 4, SHARD, NARROW),
        full(2, 8, D),
        low(2, FULL, D),
        low(2, 4, ROWS, D),
        full(2, 4, ROWS, D),
        low(2, 4, ROWS, D),
        low(2, 4, ROWS, D),
        low(2, 4, 4, ROWS, D),
        low(2, 4, 4, ROWS, D),
        low(2, 4, 4, FULL, 384),
        full(4, STACK, CHUNK),
        low(2, 4, STACK, CHUNK),
        low(2, STACK, 256),
        full(STACK, 256),
        full(STACK, 1),
        full(2, STACK, 1),
        full(2, FULL, 256),
        low(2, 4, ROWS, D),
        full(2, 4, ROWS, D),
        low(2, FULL, D),
        full(2, FULL, D),
        low(2, 4, 4, FULL, 384),
        low(2, 4, 4, 64, 384),
        low(2, 4, 4, 64, 384),
        low(2, 4, 64, 384),
        low(2, 4, 64, 384),
        low(2, 4, 64, 384),
        low(2, 4, 64, 384),
        low(2, 2, 4, 4, SHARD, WIDE),
        low(2, 2, 4, 4, SHARD, NARROW),
        low(2, 2, 4, 4, SHARD, NARROW),
        low(2, 4, 4, SHARD, WIDE),
        low(2, 4, 4, SHARD, WIDE),
        low(2, 4, 4, SHARD, WIDE),
        low(2, 4, SHARD, WIDE),
        low(2, 4, SHARD, WIDE),
        full(2, SHARD, WIDE),
        full(2, SHARD, WIDE),
        low(2, 4, 4, SHARD, NARROW),
        low(2, 4, 4, SHARD, NARROW),
        low(2, 4, 4, SHARD, NARROW),
        low(2, 4, SHARD, NARROW),
        low(2, 4, SHARD, NARROW),
        full(2, SHARD, NARROW),
        full(2, SHARD, NARROW),
        low(2, 4, 4, SHARD, NARROW),
        low(2, 4, 4, SHARD, NARROW),
        low(2, 4, 4, SHARD, NARROW),
        low(2, 4, SHARD, NARROW),
        low(2, 4, SHARD, NARROW),
        full(2, SHARD, NARROW),
        full(2, SHARD, NARROW),
        full(2, 8, D),
        full(8, D),
        full(4, 8, D),
        full(4, 8, D),
        full(4, 8, D),
        low(2, ROWS, D),
        low(ROWS, D),
        low(2, ROWS, D),
        low(ROWS, D),
    ]


def result_kernel(
    acts,
    in_grads,
    wide,
    joint,
    side,
    sums,
    activations,
    input_grads,
    ln1_gain,
    ln1_bias,
    w_qkv,
    b_qv,
    w_out,
    b_out,
    ln2_gain,
    ln2_bias,
    w_up,
    b_up,
    w_down,
    b_down,
):
    activations[0] = acts[...]
    input_grads[0] = in_grads[...]
    rows = (ln1_gain, ln1_bias, b_out, ln2_gain, ln2_bias, b_down, b_up)
    for index, target in enumerate(rows):
        target[...] = sums[index : index + 1, :]
    b_qv[0, 0:1, :] = sums[7:8, 384:576]
    b_qv[0, 1:2, :] = sums[7:8, 192:384]
    w_up[0] = wide[0]
    w_down[0] = wide[1]
    w_qkv[0, 0] = side[0, :, :192]
    w_qkv[0, 1] = joint[0, :, :192]
    w_qkv[0, 2] = joint[1, :, 64:]
    w_out[0] = side[1, :, 64:]


def model_rows_first(arrays):
    arrays = list(arrays)
    for index in (4, 6, 12):
        arrays[index] = jnp.swapaxes(arrays[index], 1, 2)
    return arrays


def local(*arrays):
    arrays = model_rows_first(arrays)
    whole = pl.BlockSpec(memory_space=pltpu.VMEM)
    results = pl.pallas_call(
        kernel,
        name="layers",
        out_shape=(
            jax.ShapeDtypeStruct((2, ROWS, D), BF16),
            jax.ShapeDtypeStruct((2, ROWS, D), BF16),
            jax.ShapeDtypeStruct((2, SHARD, WIDE), F32),
            jax.ShapeDtypeStruct((2, SHARD, NARROW), F32),
            jax.ShapeDtypeStruct((2, SHARD, NARROW), F32),
            jax.ShapeDtypeStruct((8, D), F32),
        ),
        in_specs=[whole] * 14,
        out_specs=(whole,) * 6,
        scratch_shapes=scratch_shapes(),
        compiler_params=pltpu.CompilerParams(
            collective_id=0, has_side_effects=True, vmem_limit_bytes=60 * 2**20
        ),
    )(*arrays)
    rows = jax.ShapeDtypeStruct((1, 2, ROWS, D), BF16)
    shapes = [rows, rows] + [jax.ShapeDtypeStruct(a.shape, F32) for a in arrays[2:]]
    results = pl.pallas_call(
        result_kernel,
        name="results",
        out_shape=shapes,
        in_specs=[whole] * 6,
        out_specs=[whole] * 14,
    )(*results)
    return tuple(model_rows_first(results))


def solution(mesh):
    rows = P(None, ("gx", "gy"), None)
    vector = P("section", None)
    qkv = P("section", "gx", None, "gy")
    bias_qv = P("section", None, "gy")
    out = P("section", "gy", "gx")
    up = P("section", "gx", "gy")
    hidden = P("section", "gy")
    sharded = (vector, vector, qkv, bias_qv, out, vector, vector, vector, up, hidden, out, vector)
    layer_rows = P("section", None, ("gx", "gy"), None)
    return jax.shard_map(
        local,
        mesh=mesh,
        in_specs=(rows, rows) + sharded,
        out_specs=(layer_rows, layer_rows) + sharded,
        check_vma=False,
    )
```

```python
import jax
import jax.numpy as jnp
from jax import lax
from jax.experimental import pallas as pl
from jax.experimental.pallas import tpu as pltpu
from jax.sharding import PartitionSpec as P

HD = 64
EPSILON = 1e-05
MASKED = -1e30
MESH = pl.DeviceIdType.MESH
F32 = jnp.float32
BF16 = jnp.bfloat16

ROWS = 32
FULL = 128
D = 768
CHUNK = 512
HEADS = 3
STACK = HEADS * FULL

WIDE = 768
NARROW = 256
SHARD = 48
SEMS = 320
PAIR_STEPS = (1, 3, 2)
GATHER_STEPS = (1, 3, 2)


def dot_nn(a, b):
    return lax.dot_general(a, b, (((1,), (0,)), ((), ())), preferred_element_type=F32)


def dot_nt(a, b):
    return lax.dot_general(a, b, (((1,), (1,)), ((), ())), preferred_element_type=F32)


def dot_tn(a, b):
    return lax.dot_general(a, b, (((0,), (0,)), ((), ())), preferred_element_type=F32)


def norm_parts(values, gain, offset):
    average = jnp.mean(values, axis=-1, keepdims=True)
    centered = values - average
    variance = jnp.mean(centered * centered, axis=-1, keepdims=True)
    factor = lax.rsqrt(variance + EPSILON)
    unit_rows = centered * factor
    return (unit_rows * gain + offset, unit_rows, factor)


def norm_back(grad_rows, unit_rows, factor, gain):
    scaled = grad_rows * gain
    first_mean = jnp.mean(scaled, axis=-1, keepdims=True)
    second_mean = jnp.mean(scaled * unit_rows, axis=-1, keepdims=True)
    return factor * (scaled - first_mean - unit_rows * second_mean)


def gelu_parts(values):
    scale = 0.7978845608028654
    inner = scale * (values + 0.044715 * values * values * values)
    bent = jnp.tanh(inner)
    active = 0.5 * values * (1.0 + bent)
    slope = 0.5 * (1.0 + bent) + 0.5 * values * (1.0 - bent * bent) * scale * (
        1.0 + 3.0 * 0.044715 * values * values
    )
    return active, slope


def column_sum(values):
    return jnp.sum(values, axis=0, keepdims=True)


def head_mask(head, first):
    lane = lax.broadcasted_iota(jnp.int32, (FULL, 256), 1)
    low = first + HD * head
    return jnp.logical_and(lane >= low, lane < low + HD)


def spread_heads(values, first):
    return jnp.concatenate(
        [jnp.where(head_mask(head, first), values, 0.0) for head in range(HEADS)], axis=0
    )


def join_heads(stacked, first):
    total = jnp.zeros((FULL, 256), F32)
    for head in range(HEADS):
        part = stacked[head * FULL : (head + 1) * FULL]
        total = total + jnp.where(head_mask(head, first), part, 0.0)
    return total


def only_if(condition, action):
    if condition is None:
        action()
    else:
        pl.when(condition)(lambda: action())


class Links:
    def __init__(self, send_sems, recv_sems):
        self.send_sems, self.recv_sems = send_sems, recv_sems
        self.count = 0
        self.sent = []
        self.section = lax.axis_index("section")
        self.row = lax.axis_index("gx")
        self.y = lax.axis_index("gy")
        self.x = self.row // 4
        self.z = self.row % 4

    def near(self, axis, steps):
        if axis == "s":
            return 1 - self.section
        return (getattr(self, axis) + (steps + 4)) % 4

    def place(self, first, second):
        s = self.section
        x = (self.x + (first + 4) * s + (second + 4) * (1 - s)) % 4
        z = (self.z + (first + 4) * (1 - s) + (second + 4) * s) % 4
        return x, z

    def device(self, axis, steps):
        s, x, z, y = self.section, self.x, self.z, self.y
        if axis == "first":
            x, z = self.place(steps, 0)
            return (s, x * 4 + z, y)
        if axis == "second":
            x, z = self.place(0, steps)
            return (s, x * 4 + z, y)
        there = self.near(axis, steps)
        if axis == "s":
            s = there
        elif axis == "x":
            x = there
        elif axis == "z":
            z = there
        else:
            y = there
        return (s, x * 4 + z, y)

    def exchange(self, axis, steps, source, target, landing, send_if=None, come_if=None):
        index = self.count
        self.count += 1
        sems = (self.send_sems.at[index], self.recv_sems.at[index])
        copy = pltpu.make_async_remote_copy(
            source, target, *sems, device_id=self.device(axis, steps), device_id_type=MESH
        )
        only_if(send_if, copy.start)
        self.sent.append((send_if, copy.wait_send))
        arrival = pltpu.make_async_remote_copy(
            landing, landing, *sems, device_id=self.device(axis, -steps), device_id_type=MESH
        )
        return lambda: only_if(come_if, arrival.wait_recv)

    def barrier(self):
        barrier = pltpu.get_barrier_semaphore()
        peers = [("s", 1)] + [(axis, steps) for axis in "xyz" for steps in (1, 2, 3)]
        for axis, steps in peers:
            pl.semaphore_signal(
                barrier, inc=1, device_id=self.device(axis, steps), device_id_type=MESH
            )
        pl.semaphore_wait(barrier, len(peers))

    def finish(self):
        for condition, wait in self.sent:
            only_if(condition, wait)
        self.sent = []


def wait_all(waits):
    for wait in waits:
        wait()


def gather_y(links, buffer):
    y = links.y
    return [
        links.exchange("y", steps, buffer.at[y], buffer.at[y], buffer.at[links.near("y", -steps)])
        for steps in GATHER_STEPS
    ]


def scatter_y(links, outgoing, incoming, partial):
    y = links.y
    outgoing[...] = partial.astype(BF16).reshape(4, ROWS, D)
    waits = [
        links.exchange(
            "y",
            steps,
            outgoing.at[links.near("y", steps)],
            incoming.at[y],
            incoming.at[links.near("y", -steps)],
        )
        for steps in (2, 1, 3)
    ]
    incoming[y] = outgoing[y]
    return waits


def sum_slots(buffer):
    total = buffer[0].astype(F32)
    for slot in range(1, 4):
        total = total + buffer[slot].astype(F32)
    return total


SCHEDULE = {
    "x": ("q0.begin", "q0.own"),
    "f0_q": ("q0.forward", "w0.begin", "w0.own"),
    "f0_kv": ("q0.cross", "w0.forward"),
    "f0_rs1": ("w0.cross", "k1.begin", "k1.own"),
    "f0_ag2": ("k1.forward", "q1.begin", "q1.own", "w1.begin", "w1.own"),
    "f0_rs2": ("k1.cross", "q1.forward", "w1.forward"),
    "f1_q": ("q1.cross",),
    "f1_rs1": ("w1.cross",),
    "b1_kv1": ("W1.begin", "Q1.begin"),
    "b1_rs2": ("K1.begin", "W1.first"),
    "b0_ag": ("Q1.first", "K1.first"),
    "b0_rs1": ("W0.begin", "W1.second"),
    "b0_ag2": ("W0.first", "Q1.second", "K1.second"),
    "b0_kv1": ("Q0.begin",),
    "b0_kv2": ("W0.second", "Q0.first", "W1.last", "Q1.last", "K1.last"),
    "b0_rs2": ("W0.last", "Q0.second"),
}
RELAYED = ()


class Gather:
    def __init__(self, links, buffer, layer, relayed):
        self.links, self.buffer, self.layer = links, buffer, layer
        self.relayed = relayed
        self.near = []
        self.far = []

    def block(self, first, second):
        x, z = self.links.place(first, second)
        return self.buffer.at[self.layer, self.links.section, x, z]

    def begin(self):
        own = self.block(0, 0)
        self.first = [
            self.links.exchange("first", steps, own, own, self.block(-steps, 0))
            for steps in (1, 3, 2)
        ]

    def send(self, first):
        came = self.block(-first, 0)
        for steps in (1, 3) if self.relayed else (1, 3, 2):
            wait = self.links.exchange("second", steps, came, came, self.block(-first, -steps))
            (self.near if steps != 2 else self.far).append(wait)

    def own(self):
        self.send(0)

    def forward(self):
        for wait, first in zip(self.first, (1, 3, 2)):
            wait()
            self.send(first)

    def relay(self):
        wait_all(self.near)
        self.near = []
        if self.relayed:
            for first, steps in zip((0, 1, 3, 2), (1, 3, 1, 3)):
                came = self.block(-first, -steps)
                self.far.append(
                    self.links.exchange("second", steps, came, came, self.block(-first, -2))
                )

    def cross(self):
        wait_all(self.near + self.far)
        s = self.links.section
        mine = self.buffer.at[self.layer, s]
        self.finish = self.links.exchange("s", 1, mine, mine, self.buffer.at[self.layer, 1 - s])


class Scatter:
    def __init__(self, links, layer, grads, crossed, work, arrived, middle, ended, done, other):
        self.links, self.layer, self.grads, self.crossed = links, layer, grads, crossed
        self.work, self.arrived, self.middle, self.ended = work, arrived, middle, ended
        self.done, self.other = done.at[layer], other.at[layer]
        s, x, z = links.section, links.x, links.z
        self.first_index = z * (1 - s) + x * s
        self.second_index = x * (1 - s) + z * s

    def begin(self):
        s = self.links.section
        self.crossing = self.links.exchange(
            "s", 1, self.grads.at[self.layer, 1 - s], self.crossed, self.crossed
        )

    def spread(self, axis, index, source, target):
        waits = []
        for steps in (2, 1, 3):
            waits.append(
                self.links.exchange(
                    axis,
                    steps,
                    source.at[(index + steps) % 4],
                    target.at[index],
                    target.at[(index + 4 - steps) % 4],
                )
            )
        target[index] = source[index]
        return waits

    def first(self):
        self.crossing()
        s = self.links.section

        def add(first, carry):
            for second in range(4):
                x = first * s + second * (1 - s)
                z = first * (1 - s) + second * s
                mine = self.grads[self.layer, s, x, z].astype(F32)
                self.work[first, second] = (mine + self.crossed[x, z].astype(F32)).astype(BF16)
            return carry

        lax.fori_loop(0, 4, add, 0)
        self.waits = self.spread("first", self.first_index, self.work, self.arrived)

    def second(self):
        wait_all(self.waits)
        self.middle[...] = sum_slots(self.arrived).astype(BF16)
        self.waits = self.spread("second", self.second_index, self.middle, self.ended)

    def last(self):
        wait_all(self.waits)
        self.done[...] = sum_slots(self.ended)
        self.finish = self.links.exchange("s", 1, self.done, self.other, self.other)


def kernel(
    inputs,
    cotangent,
    ln1_gain,
    ln1_bias,
    w_qkv,
    b_qv,
    w_out,
    b_out,
    ln2_gain,
    ln2_bias,
    w_up,
    b_up,
    w_down,
    b_down,
    activations,
    input_grads,
    wide_out,
    joint_out,
    side_out,
    param_grads,
    send_sems,
    recv_sems,
    own_wide,
    own_joint,
    own_side,
    wide,
    joint,
    side,
    params,
    normed_one,
    normed_two,
    units,
    grad_outs,
    grad_branches,
    scatter_out,
    scatter_in,
    pairs,
    scores,
    probs,
    queries,
    query_sums,
    tops,
    totals,
    attended,
    hidden,
    middles,
    actives,
    slopes,
    pair_grads,
    pair_in_a,
    pair_in_b,
    pair_mid_a,
    pair_mid_b,
    pair_end_a,
    pair_end_b,
    wide_grads,
    joint_grads,
    side_grads,
    wide_crossed,
    wide_work,
    wide_arrived,
    wide_middle,
    wide_ended,
    wide_done,
    wide_other,
    joint_crossed,
    joint_work,
    joint_arrived,
    joint_middle,
    joint_ended,
    joint_done,
    joint_other,
    side_crossed,
    side_work,
    side_arrived,
    side_middle,
    side_ended,
    side_done,
    side_other,
    sums,
    sums_cross,
    sums_y,
    sums_z,
    sums_x,
    outputs,
    output_cross,
    in_grads,
    in_grad_cross,
):
    links = Links(send_sems, recv_sems)
    s, x, z, y, row = links.section, links.x, links.z, links.y, links.row
    other = 1 - s
    own_wide[0] = w_up[0]
    own_wide[1] = w_down[0]
    none = jnp.zeros((SHARD, 64), BF16)
    own_joint[0] = jnp.concatenate([w_qkv[0, 1], none], axis=1)
    own_joint[1] = jnp.concatenate([none, w_qkv[0, 2]], axis=1)
    own_side[0] = jnp.concatenate([w_qkv[0, 0], none], axis=1)
    own_side[1] = jnp.concatenate([none, w_out[0]], axis=1)
    rows = (ln1_gain, ln1_bias, b_out, ln2_gain, ln2_bias, b_down, b_up)
    for index, values in enumerate(rows):
        params[s, index : index + 1, :] = values[...]
    blank = jnp.zeros((1, 192), F32)
    params[s, 7:8, :] = jnp.concatenate([blank, b_qv[0, 1:2], b_qv[0, 0:1], blank], axis=1)
    wide[s, :, x, z] = own_wide[...]
    joint[s, :, x, z] = own_joint[...]
    side[s, :, x, z] = own_side[...]
    links.barrier()

    joint_wait = links.exchange(
        "s", 1, own_joint.at[other], joint.at[s, other, x, z], joint.at[other, s, x, z]
    )
    params_wait = links.exchange("s", 1, params.at[s], params.at[s], params.at[other])
    side_wait = links.exchange(
        "s", 1, own_side.at[other], side.at[s, other, x, z], side.at[other, s, x, z]
    )
    wide_wait = links.exchange(
        "s", 1, own_wide.at[other], wide.at[s, other, x, z], wide.at[other, s, x, z]
    )
    tasks = {}
    for layer in range(2):
        for name, buffer in (("k", joint), ("q", side), ("w", wide)):
            name = name + str(layer)
            tasks[name] = Gather(links, buffer, layer, name in RELAYED)

    def slot(name):
        for step in SCHEDULE.get(name, ()):
            task, action = step.split(".")
            getattr(tasks[task], action)()

    joint_wait()
    tasks["k0"].begin()
    tasks["k0"].own()
    params_wait()

    def gather_hidden(layer, current):
        hidden[layer, y] = current
        waits = gather_y(links, hidden.at[layer])
        slot(f"f{layer}_ag")
        return waits

    hidden_waits = gather_hidden(0, inputs[s])

    side_wait()
    wide_wait()
    tasks["k0"].forward()
    slot("w")
    tasks["k0"].relay()
    tasks["k0"].cross()
    slot("x")

    def matrix(buffer, layer, half):
        return buffer[layer, half].reshape(D, buffer.shape[-1])

    def gather_grads(layer, grad_rows):
        grad_outs[layer, y] = grad_rows
        return gather_y(links, grad_outs.at[layer])

    cotangent_waits = []

    def forward(layer, hidden_waits):
        wait_all(hidden_waits)
        hidden_full = hidden[layer].reshape(FULL, D).astype(F32)
        normed, unit_rows, _ = norm_parts(hidden_full, params[layer, 0:1, :], params[layer, 1:2, :])
        normed = normed.astype(BF16)
        normed_one[layer] = normed
        units[layer] = unit_rows.reshape(4, ROWS, D)
        tasks[f"k{layer}"].finish()
        key = dot_nn(normed, matrix(joint, layer, 0))
        value = dot_nn(normed, matrix(joint, layer, 1))
        pair = jnp.concatenate(
            [key[:, :128], key[:, 128:] + value[:, :128], value[:, 128:]], axis=1
        )
        pair = pair + params[layer, 7:8, 0:384]
        pairs[layer, x, z] = pair.astype(BF16)
        own = pairs.at[layer]
        low, high = pl.ds(0, 64), pl.ds(64, 64)
        pair_waits = {steps: [] for steps in range(4)}

        def pairs_x(column, half):
            for steps in PAIR_STEPS:
                yield steps, links.exchange(
                    "x",
                    steps,
                    own.at[x, column, half],
                    own.at[x, column, half],
                    own.at[links.near("x", -steps), column, half],
                    x <= 3 - steps,
                    x >= steps,
                )

        def pairs_z(plane, half, condition):
            for steps in (1, 3, 2):
                yield steps, links.exchange(
                    "z",
                    steps,
                    own.at[plane, z, half],
                    own.at[plane, z, half],
                    own.at[plane, links.near("z", -steps), half],
                    condition,
                    condition,
                )

        pair_first_a = list(pairs_z(x, low, None))
        pair_first_b = list(pairs_x(z, high))
        for steps, wait in pairs_x(z, low):
            pair_waits[steps].append(wait)
        pair_waits[0] += [wait for _, wait in pairs_z(x, high, None)]
        slot(f"f{layer}_q")
        for (steps_a, wait_a), (steps_b, wait_b) in zip(pair_first_a, pair_first_b):
            wait_a()
            for steps, wait in pairs_x(links.near("z", -steps_a), low):
                pair_waits[steps].append(wait)
            wait_b()
            came = links.near("x", -steps_b)
            pair_waits[steps_b] += [wait for _, wait in pairs_z(came, high, x >= steps_b)]
        if layer == 0:
            cotangent_waits.extend(gather_grads(1, cotangent[s]))
        slot(f"f{layer}_kv")
        tasks[f"q{layer}"].finish()
        query = dot_nn(normed, matrix(side, layer, 0)) + params[layer, 7:8, 384:640]
        query = query.astype(BF16).astype(F32) * 0.125
        queries[layer] = spread_heads(query, 0).astype(BF16)

        stacked = queries[layer]
        position = lax.broadcasted_iota(jnp.int32, (STACK, CHUNK), 0) % FULL + row * FULL
        column = lax.broadcasted_iota(jnp.int32, (STACK, CHUNK), 1)

        def find_top(chunk):
            keys = pairs[layer, chunk, :, :, 0:256].reshape(CHUNK, 256)
            raw = dot_nt(stacked, keys)
            raw = jnp.where(column + chunk * CHUNK <= position, raw, MASKED)
            scores[chunk] = raw
            tops[...] = jnp.maximum(tops[...], jnp.max(raw, axis=1, keepdims=True))

        tops[...] = jnp.full((STACK, 1), MASKED, F32)
        for steps in (0, 1, 3, 2):
            wait_all(pair_waits[steps])
            chunk = links.near("x", -steps)
            only_if(None if steps == 0 else x >= steps, lambda: find_top(chunk))
        top = tops[...]

        def add_chunk(chunk, carry):
            total, summed = carry
            weight = jnp.exp(scores[chunk] - top)
            rounded = weight.astype(BF16)
            probs[layer, chunk] = rounded
            values = pairs[layer, chunk, :, :, 128:384].reshape(CHUNK, 256)
            return (
                total + jnp.sum(weight, axis=1, keepdims=True),
                summed + dot_nn(rounded, values),
            )

        total, summed = lax.fori_loop(
            0, x + 1, add_chunk, (jnp.zeros((STACK, 1), F32), jnp.zeros((STACK, 256), F32))
        )
        totals[layer] = total
        attention = join_heads(summed / total, HD)
        attended[layer] = attention
        partial = dot_nt(attention.astype(BF16), matrix(side, layer, 1))
        waits = scatter_y(links, scatter_out.at[layer, 0], scatter_in.at[layer, 0], partial)
        slot(f"f{layer}_rs1")
        wait_all(waits)
        middle = hidden[layer, y].astype(F32) + sum_slots(scatter_in.at[layer, 0])
        middle = middle + params[layer, 2:3, :]
        middles[layer, y] = middle
        second, _, _ = norm_parts(middle, params[layer, 3:4, :], params[layer, 4:5, :])
        normed_two[layer, y] = second.astype(BF16)
        waits = gather_y(links, normed_two.at[layer])
        slot(f"f{layer}_ag2")
        wait_all(waits)
        tasks[f"w{layer}"].finish()
        upward = (
            dot_nn(normed_two[layer].reshape(FULL, D), matrix(wide, layer, 0)) + params[layer, 6:7, :]
        )
        active, slope = gelu_parts(upward)
        actives[layer] = active.astype(BF16)
        slopes[layer] = slope
        partial = dot_nt(actives[layer], matrix(wide, layer, 1))
        waits = scatter_y(links, scatter_out.at[layer, 1], scatter_in.at[layer, 1], partial)
        slot(f"f{layer}_rs2")
        wait_all(waits)
        result = middles[layer, y] + sum_slots(scatter_in.at[layer, 1]) + params[layer, 5:6, :]
        outputs[layer] = result.astype(BF16)

    forward(0, hidden_waits)
    forward(1, gather_hidden(1, outputs[0]))
    output_wait = links.exchange("s", 1, outputs.at[other], output_cross, output_cross)

    def scatters(layer):
        wide_scatter = Scatter(
            links,
            layer,
            wide_grads,
            wide_crossed.at[layer],
            wide_work.at[layer],
            wide_arrived.at[layer],
            wide_middle.at[layer],
            wide_ended.at[layer],
            wide_done,
            wide_other,
        )
        joint_scatter = Scatter(
            links,
            layer,
            joint_grads,
            joint_crossed.at[layer],
            joint_work.at[layer],
            joint_arrived.at[layer],
            joint_middle.at[layer],
            joint_ended.at[layer],
            joint_done,
            joint_other,
        )
        side_scatter = Scatter(
            links,
            layer,
            side_grads,
            side_crossed.at[layer],
            side_work.at[layer],
            side_arrived.at[layer],
            side_middle.at[layer],
            side_ended.at[layer],
            side_done,
            side_other,
        )
        return wide_scatter, joint_scatter, side_scatter

    for layer in range(2):
        tasks[f"W{layer}"], tasks[f"K{layer}"], tasks[f"Q{layer}"] = scatters(layer)

    sum_waits = []

    def backward(layer, waits):
        grad_rows = grad_outs[layer, y]
        sums[layer, 5:6, :] = column_sum(grad_rows.astype(F32))
        gain_one, gain_two = params[layer, 0:1, :], params[layer, 3:4, :]
        _, unit_one, factor_one = norm_parts(hidden[layer, y].astype(F32), gain_one, gain_one)
        _, unit_two, factor_two = norm_parts(middles[layer, y], gain_two, gain_two)
        slot(f"b{layer}_ag")
        wait_all(waits)
        grad_full = grad_outs[layer].reshape(FULL, D)
        grad_up = (dot_nn(grad_full, matrix(wide, layer, 1)) * slopes[layer]).astype(BF16)
        partial = dot_nt(grad_up, matrix(wide, layer, 0))
        waits = scatter_y(links, scatter_out.at[layer, 2], scatter_in.at[layer, 2], partial)
        down_grad = dot_tn(grad_full, actives[layer])
        wide_grads[layer, 1] = down_grad.astype(BF16).reshape(4, 4, SHARD, WIDE)
        up_grad = dot_tn(normed_two[layer].reshape(FULL, D), grad_up)
        wide_grads[layer, 0] = up_grad.astype(BF16).reshape(4, 4, SHARD, WIDE)
        sums[layer, 6:7, :] = column_sum(grad_up.astype(F32))
        slot(f"b{layer}_rs1")
        wait_all(waits)
        grad_two = sum_slots(scatter_in.at[layer, 2])
        grad_middle = grad_rows.astype(F32) + norm_back(grad_two, unit_two, factor_two, gain_two)
        grad_branches[layer, y] = grad_middle.astype(BF16)
        waits = gather_y(links, grad_branches.at[layer])
        sums[layer, 2:3, :] = column_sum(grad_middle)
        sums[layer, 3:4, :] = column_sum(grad_two * unit_two)
        sums[layer, 4:5, :] = column_sum(grad_two)
        slot(f"b{layer}_ag2")
        wait_all(waits)
        branch_full = grad_branches[layer].reshape(FULL, D)
        grad_mixed = dot_nn(branch_full, matrix(side, layer, 1)).astype(BF16).astype(F32)
        stacked_grad = spread_heads(grad_mixed, HD)
        delta = jnp.sum(spread_heads(grad_mixed * attended[layer], HD), axis=1, keepdims=True)
        inverse = 1.0 / totals[layer]
        scaled_grad = (stacked_grad * inverse).astype(BF16)
        stacked_grad = stacked_grad.astype(BF16)
        stacked = queries[layer]

        own = pair_grads.at[layer]
        low, high = pl.ds(0, 64), pl.ds(64, 64)
        waits_a, waits_b = [], []

        def chunk_back(chunk):
            keys = pairs[layer, chunk, :, :, 0:256].reshape(CHUNK, 256)
            values = pairs[layer, chunk, :, :, 128:384].reshape(CHUNK, 256)
            weight = probs[layer, chunk]
            products = dot_nt(stacked_grad, values)
            score_grad = (weight.astype(F32) * (products - delta) * inverse).astype(BF16)
            key_grad = dot_tn(score_grad, stacked)
            value_grad = dot_tn(weight, scaled_grad)
            joined = jnp.concatenate(
                [
                    key_grad[:, :128],
                    key_grad[:, 128:] + value_grad[:, :128],
                    value_grad[:, 128:],
                ],
                axis=1,
            )
            pair_grads[layer, chunk] = joined.astype(BF16).reshape(4, FULL, 384)
            pair_in_b[layer, z, chunk] = pair_grads[layer, chunk, z, 64:128]
            query_sums[...] = query_sums[...] + dot_nn(score_grad, keys)

        def earlier(chunk):
            chunk_back(chunk)
            pair_in_a[layer, chunk] = jnp.zeros((4, 64, 384), BF16)
            pair_end_b[layer, chunk] = jnp.zeros((64, 384), BF16)

        def send_z(chunk, condition):
            for steps in (2, 1, 3):
                waits_b.append(
                    links.exchange(
                        "z",
                        steps,
                        own.at[chunk, links.near("z", steps), high],
                        pair_in_b.at[layer, z, chunk],
                        pair_in_b.at[layer, links.near("z", -steps), chunk],
                        condition,
                        condition,
                    )
                )

        query_sums[...] = jnp.zeros((STACK, 256), F32)
        for steps in (3, 2, 1):
            chunk = links.near("x", -steps)
            pl.when(x >= steps)(lambda: earlier(chunk))
            waits_a.append(
                links.exchange(
                    "x",
                    -steps,
                    own.at[chunk, :, low],
                    pair_in_a.at[layer, x],
                    pair_in_a.at[layer, links.near("x", steps)],
                    x >= steps,
                    x <= 3 - steps,
                )
            )
            send_z(chunk, x >= steps)
        chunk_back(x)
        send_z(x, None)
        pair_in_a[layer, x] = pair_grads[layer, x, :, 0:64]
        query_sum = query_sums[...]
        grad_query = (join_heads(query_sum, 0) * 0.125).astype(BF16)
        normed = normed_one[layer]
        query_grad = dot_tn(normed, grad_query)
        side_grads[layer, 0] = query_grad.astype(BF16).reshape(4, 4, SHARD, NARROW)
        out_grad = dot_tn(branch_full, attended[layer].astype(BF16))
        side_grads[layer, 1] = out_grad.astype(BF16).reshape(4, 4, SHARD, NARROW)
        partial = dot_nt(grad_query, matrix(side, layer, 0))
        slot(f"b{layer}_kv1")
        wait_all(waits_a)
        pair_mid_a[layer] = sum_slots(pair_in_a.at[layer]).astype(BF16)
        waits_a = [
            links.exchange(
                "z",
                steps,
                pair_mid_a.at[layer, links.near("z", steps)],
                pair_end_a.at[layer, z],
                pair_end_a.at[layer, links.near("z", -steps)],
            )
            for steps in (2, 1, 3)
        ]
        pair_end_a[layer, z] = pair_mid_a[layer, z]
        wait_all(waits_b)

        def sum_chunk(chunk):
            pair_mid_b[layer, chunk] = sum_slots(pair_in_b.at[layer, :, chunk]).astype(BF16)

        waits_b = []
        for steps in (3, 2, 1):
            chunk = links.near("x", -steps)
            pl.when(x >= steps)(lambda: sum_chunk(chunk))
            waits_b.append(
                links.exchange(
                    "x",
                    -steps,
                    pair_mid_b.at[layer, chunk],
                    pair_end_b.at[layer, x],
                    pair_end_b.at[layer, links.near("x", steps)],
                    x >= steps,
                    x <= 3 - steps,
                )
            )
        sum_chunk(x)
        pair_end_b[layer, x] = pair_mid_b[layer, x]
        slot(f"b{layer}_kv2")
        wait_all(waits_a)
        wait_all(waits_b)
        grad_pair = jnp.concatenate(
            [sum_slots(pair_end_a.at[layer]), sum_slots(pair_end_b.at[layer])], axis=0
        ).astype(BF16)
        def joint_gradients():
            key_weight_grad = dot_tn(normed, grad_pair[:, 0:256])
            joint_grads[layer, 0] = key_weight_grad.astype(BF16).reshape(4, 4, SHARD, NARROW)
            value_weight_grad = dot_tn(normed, grad_pair[:, 128:384])
            joint_grads[layer, 1] = value_weight_grad.astype(BF16).reshape(4, 4, SHARD, NARROW)

        if layer == 0:
            joint_gradients()
            tasks["K0"].begin()
        partial = partial + dot_nt(grad_pair[:, 0:256], matrix(joint, layer, 0))
        partial = partial + dot_nt(grad_pair[:, 128:384], matrix(joint, layer, 1))
        waits = scatter_y(links, scatter_out.at[layer, 3], scatter_in.at[layer, 3], partial)
        if layer == 1:
            joint_gradients()
        sums[layer, 0:1, :] = column_sum(partial * units[layer].reshape(FULL, D))
        sums[layer, 1:2, :] = column_sum(partial)
        sums[layer, 7:8, :] = jnp.concatenate(
            [
                column_sum(grad_pair.astype(F32)),
                column_sum(grad_query.astype(F32)),
                jnp.zeros((1, 128), F32),
            ],
            axis=1,
        )
        slot(f"b{layer}_rs2")
        if layer == 0:
            sums_wait = links.exchange("s", 1, sums.at[other], sums_cross, sums_cross)
            sums_wait()
            sums_y[y] = sums[s] + sums_cross[...]
            sum_waits.extend(gather_y(links, sums_y))
            tasks["K0"].first()
        wait_all(waits)
        grad_one = sum_slots(scatter_in.at[layer, 3])
        grad_input = grad_middle + norm_back(grad_one, unit_one, factor_one, gain_one)
        in_grads[layer] = grad_input.astype(BF16)

    backward(1, cotangent_waits)
    backward(0, gather_grads(0, in_grads[1]))
    in_grad_wait = links.exchange("s", 1, in_grads.at[other], in_grad_cross, in_grad_cross)

    output_wait()
    activations[s] = outputs[s]
    activations[other] = output_cross[...]
    wait_all(sum_waits)
    sums_z[z] = jnp.concatenate([sum_slots(sums_y)[0:6], sums_y[y, 6:8, :]], axis=0)
    waits = [
        links.exchange(
            "z", steps, sums_z.at[z], sums_z.at[z], sums_z.at[links.near("z", -steps)]
        )
        for steps in (1, 3, 2)
    ]
    tasks["Q0"].last()
    tasks["K0"].second()
    in_grad_wait()
    input_grads[s] = in_grads[s]
    input_grads[other] = in_grad_cross[...]
    wait_all(waits)
    sums_x[x] = sum_slots(sums_z)
    waits = [
        links.exchange(
            "x", steps, sums_x.at[x], sums_x.at[x], sums_x.at[links.near("x", -steps)]
        )
        for steps in (1, 3, 2)
    ]
    tasks["K0"].last()
    wait_all(waits)
    param_grads[...] = sum_slots(sums_x)
    for layer in range(2):
        tasks[f"W{layer}"].finish()
        tasks[f"K{layer}"].finish()
        tasks[f"Q{layer}"].finish()
    wide_out[s] = wide_done[s]
    wide_out[other] = wide_other[s]
    joint_out[s] = joint_done[s]
    joint_out[other] = joint_other[s]
    side_out[s] = side_done[s]
    side_out[other] = side_other[s]
    links.finish()


def scratch_shapes():
    def low(*shape):
        return pltpu.VMEM(shape, BF16)

    def full(*shape):
        return pltpu.VMEM(shape, F32)

    return [
        pltpu.SemaphoreType.DMA((SEMS,)),
        pltpu.SemaphoreType.DMA((SEMS,)),
        low(2, SHARD, WIDE),
        low(2, SHARD, NARROW),
        low(2, SHARD, NARROW),
        low(2, 2, 4, 4, SHARD, WIDE),
        low(2, 2, 4, 4, SHARD, NARROW),
        low(2, 2, 4, 4, SHARD, NARROW),
        full(2, 8, D),
        low(2, FULL, D),
        low(2, 4, ROWS, D),
        full(2, 4, ROWS, D),
        low(2, 4, ROWS, D),
        low(2, 4, ROWS, D),
        low(2, 4, 4, ROWS, D),
        low(2, 4, 4, ROWS, D),
        low(2, 4, 4, FULL, 384),
        full(4, STACK, CHUNK),
        low(2, 4, STACK, CHUNK),
        low(2, STACK, 256),
        full(STACK, 256),
        full(STACK, 1),
        full(2, STACK, 1),
        full(2, FULL, 256),
        low(2, 4, ROWS, D),
        full(2, 4, ROWS, D),
        low(2, FULL, D),
        full(2, FULL, D),
        low(2, 4, 4, FULL, 384),
        low(2, 4, 4, 64, 384),
        low(2, 4, 4, 64, 384),
        low(2, 4, 64, 384),
        low(2, 4, 64, 384),
        low(2, 4, 64, 384),
        low(2, 4, 64, 384),
        low(2, 2, 4, 4, SHARD, WIDE),
        low(2, 2, 4, 4, SHARD, NARROW),
        low(2, 2, 4, 4, SHARD, NARROW),
        low(2, 4, 4, SHARD, WIDE),
        low(2, 4, 4, SHARD, WIDE),
        low(2, 4, 4, SHARD, WIDE),
        low(2, 4, SHARD, WIDE),
        low(2, 4, SHARD, WIDE),
        full(2, SHARD, WIDE),
        full(2, SHARD, WIDE),
        low(2, 4, 4, SHARD, NARROW),
        low(2, 4, 4, SHARD, NARROW),
        low(2, 4, 4, SHARD, NARROW),
        low(2, 4, SHARD, NARROW),
        low(2, 4, SHARD, NARROW),
        full(2, SHARD, NARROW),
        full(2, SHARD, NARROW),
        low(2, 4, 4, SHARD, NARROW),
        low(2, 4, 4, SHARD, NARROW),
        low(2, 4, 4, SHARD, NARROW),
        low(2, 4, SHARD, NARROW),
        low(2, 4, SHARD, NARROW),
        full(2, SHARD, NARROW),
        full(2, SHARD, NARROW),
        full(2, 8, D),
        full(8, D),
        full(4, 8, D),
        full(4, 8, D),
        full(4, 8, D),
        low(2, ROWS, D),
        low(ROWS, D),
        low(2, ROWS, D),
        low(ROWS, D),
    ]


def result_kernel(
    acts,
    in_grads,
    wide,
    joint,
    side,
    sums,
    activations,
    input_grads,
    ln1_gain,
    ln1_bias,
    w_qkv,
    b_qv,
    w_out,
    b_out,
    ln2_gain,
    ln2_bias,
    w_up,
    b_up,
    w_down,
    b_down,
):
    activations[0] = acts[...]
    input_grads[0] = in_grads[...]
    rows = (ln1_gain, ln1_bias, b_out, ln2_gain, ln2_bias, b_down, b_up)
    for index, target in enumerate(rows):
        target[...] = sums[index : index + 1, :]
    b_qv[0, 0:1, :] = sums[7:8, 384:576]
    b_qv[0, 1:2, :] = sums[7:8, 192:384]
    w_up[0] = wide[0]
    w_down[0] = wide[1]
    w_qkv[0, 0] = side[0, :, :192]
    w_qkv[0, 1] = joint[0, :, :192]
    w_qkv[0, 2] = joint[1, :, 64:]
    w_out[0] = side[1, :, 64:]


def model_rows_first(arrays):
    arrays = list(arrays)
    for index in (4, 6, 12):
        arrays[index] = jnp.swapaxes(arrays[index], 1, 2)
    return arrays


def local(*arrays):
    arrays = model_rows_first(arrays)
    whole = pl.BlockSpec(memory_space=pltpu.VMEM)
    results = pl.pallas_call(
        kernel,
        name="layers",
        out_shape=(
            jax.ShapeDtypeStruct((2, ROWS, D), BF16),
            jax.ShapeDtypeStruct((2, ROWS, D), BF16),
            jax.ShapeDtypeStruct((2, SHARD, WIDE), F32),
            jax.ShapeDtypeStruct((2, SHARD, NARROW), F32),
            jax.ShapeDtypeStruct((2, SHARD, NARROW), F32),
            jax.ShapeDtypeStruct((8, D), F32),
        ),
        in_specs=[whole] * 14,
        out_specs=(whole,) * 6,
        scratch_shapes=scratch_shapes(),
        compiler_params=pltpu.CompilerParams(
            collective_id=0, has_side_effects=True, vmem_limit_bytes=60 * 2**20
        ),
    )(*arrays)
    rows = jax.ShapeDtypeStruct((1, 2, ROWS, D), BF16)
    shapes = [rows, rows] + [jax.ShapeDtypeStruct(a.shape, F32) for a in arrays[2:]]
    results = pl.pallas_call(
        result_kernel,
        name="results",
        out_shape=shapes,
        in_specs=[whole] * 6,
        out_specs=[whole] * 14,
    )(*results)
    return tuple(model_rows_first(results))


def solution(mesh):
    rows = P(None, ("gx", "gy"), None)
    vector = P("section", None)
    qkv = P("section", "gx", None, "gy")
    bias_qv = P("section", None, "gy")
    out = P("section", "gy", "gx")
    up = P("section", "gx", "gy")
    hidden = P("section", "gy")
    sharded = (vector, vector, qkv, bias_qv, out, vector, vector, vector, up, hidden, out, vector)
    layer_rows = P("section", None, ("gx", "gy"), None)
    return jax.shard_map(
        local,
        mesh=mesh,
        in_specs=(rows, rows) + sharded,
        out_specs=(layer_rows, layer_rows) + sharded,
        check_vma=False,
    )
```
